128 devices in a mesh: hid: 8 (over z, x_hi), wid: 16 (over y, x_lo, core).
Axes of the slice: x: 4 (x_hi: 2, x_lo: 2; x = x_hi * 2 + x_lo), y: 4, z: 4, core: 2. Of those that a mesh axis runs over, the one named last changes fastest.
Arguments:
- spec_rows: int32 [1024, 2], replicated, may hold values from 0 to 2047, as said below
- readout: bfloat16 [2048, 8192], P(None, 'wid'), may hold values from -6 to 6
- gate_weight: bfloat16 [8192, 28672], P('wid', 'hid'), may hold values from -0.0625 to 0.0625
- up_weight: bfloat16 [8192, 28672], P('wid', 'hid'), may hold values from -0.0625 to 0.0625
- down_weight: bfloat16 [28672, 8192], P('hid', 'wid'), may hold values from -0.03125 to 0.03125
- gate_lo: float32 [28672], P('hid'), may hold values from -6 to 6
- gate_width: float32 [28672], P('hid'), may hold values from 0.5 to 4
- up_lo: float32 [28672], P('hid'), may hold values from -6 to 6
- up_width: float32 [28672], P('hid'), may hold values from 0.5 to 4
- flags: int32 [28672], P('hid'), may hold values 0 or 1
Outputs:
- input_coeffs: float32 [1024, 8192], P('hid', 'wid')
- offsets: float32 [1024], P('wid')
The draws below stay inside these ranges and needn't reach their ends.
Inputs may be any that keep to these rules, and one draw needn't show every extreme that they name: `spec_rows`: each row names two different classes; every class is named by exactly one entry of one row.
All inputs are finite; a program needn't handle non-finite values. No bound on the sum of `flags` on one device may be relied on, other than what follows from the above.
Results may differ from the reference program's by a relative error of at most 0.0041.
Values may be sent and summed in bfloat16 or wider, within the bound.
A program may use at most 128 MiB of HBM per device.

```python
import math
import jax
import jax.numpy as jnp
from jax import lax

D = 8192
FF = 28672
S_ROWS = 1024
CLASSES = 2048


def draw_spec_rows(key, part):
    key = jax.random.fold_in(key, 7)
    order = jax.random.permutation(key, CLASSES).astype(jnp.int32)
    target = order[:S_ROWS]
    rival = order[S_ROWS:]
    return jnp.stack([target, rival], axis=1).astype(jnp.int32)


def place_ends(entries, rng, low, high):
    extent = entries.shape
    place = [jax.random.randint(jax.random.fold_in(rng, axis), (), 0, extent[axis]) for axis in range(len(extent))]
    entries = entries.at[tuple(place)].set(low)
    longest = extent.index(max(extent))
    place[longest] = (place[longest] + 1) % extent[longest]
    return entries.at[tuple(place)].set(high)


def block_levels(key, shape, pieces, least, high):
    loudness, own = 1.0, jax.random.fold_in(key, 6)
    for position, shards_of in pieces:
        steps = jnp.exp(jax.random.uniform(jax.random.fold_in(own, position), (shards_of,), jnp.float32, least / len(pieces), high / len(pieces)))
        loudness = loudness * jnp.repeat(steps, shape[position] // shards_of).reshape([-1 if axis == position else 1 for axis in range(len(shape))])
    return loudness


def bell_draw(own_key, shape, spread, limit, cuts=(), held_as=jnp.bfloat16):
    level = block_levels(own_key, shape, cuts, -0.22, 0.18) if cuts else 1.0
    values = jax.random.normal(own_key, shape, jnp.float32) * spread * level
    return jnp.minimum(jnp.maximum(values, -limit), limit).astype(held_as)


def setup_inputs(seed: int = 0) -> dict:
    splits = jax.random.split(jax.random.key(seed), 11)
    return {
        "spec_rows": draw_spec_rows(jax.random.fold_in(splits[10], 71), 0),
        "readout": bell_draw(splits[1], (CLASSES, D), 1.0, 6.0, ((1, 16),)),
        "gate_weight": bell_draw(splits[2], (D, FF), D ** -0.5, 0.0625, ((0, 16), (1, 8))),
        "up_weight": bell_draw(splits[3], (D, FF), D ** -0.5, 0.0625, ((0, 16), (1, 8))),
        "down_weight": bell_draw(splits[4], (FF, D), FF ** -0.5, 0.03125, ((0, 8), (1, 16))),
        "gate_lo": bell_draw(splits[5], (FF,), 1.5, 6.0, ((0, 8),), jnp.float32),
        "gate_width": jnp.clip(jnp.exp(math.log(4.0) - 2.0794415 * jax.random.uniform(splits[6], (FF,), jnp.float32) ** block_levels(splits[6], (FF,), ((0, 8),), -0.2, 0.2)), 0.5, 4.0),
        "up_lo": bell_draw(splits[7], (FF,), 1.5, 6.0, ((0, 8),), jnp.float32),
        "up_width": jnp.clip(jnp.exp(math.log(4.0) - 2.0794415 * jax.random.uniform(splits[8], (FF,), jnp.float32) ** block_levels(splits[8], (FF,), ((0, 8),), -0.2, 0.2)), 0.5, 4.0),
        "flags": place_ends((jax.random.randint(splits[9], (FF,), 0, 2) < 1).astype(jnp.int32), jax.random.fold_in(splits[9], 1), 0, 1),
    }


def silu(value):
    return value / (1.0 + jnp.exp(-value))


def unit_tables(gate_lo, gate_width, up_lo, up_width, flags):
    gate_hi = gate_lo + gate_width
    up_hi = up_lo + up_width
    middle = 0.5 * (gate_lo + gate_hi)
    valley = jnp.clip(-1.2784645, gate_lo, gate_hi)
    silu_lo = silu(gate_lo)
    silu_hi = silu(gate_hi)
    s_low = jnp.minimum(jnp.minimum(silu_lo, silu_hi), silu(valley))
    s_high = jnp.maximum(silu_lo, silu_hi)
    slope = (silu_hi - silu_lo) / gate_width
    rest_a = silu_lo - slope * gate_lo
    rest_b = silu(middle) - slope * middle
    rest_c = silu(valley) - slope * valley
    b_low = jnp.minimum(jnp.minimum(rest_a, rest_b), rest_c)
    b_high = jnp.maximum(jnp.maximum(rest_a, rest_b), rest_c)
    second = flags == 1
    as_lower = jnp.where(second, up_hi, up_lo)
    au_lower = jnp.where(second, s_high, s_low)
    c_lower = jnp.where(second, -s_high * up_hi, -s_low * up_lo)
    as_upper = jnp.where(second, up_lo, up_hi)
    au_upper = jnp.where(second, s_high, s_low)
    c_upper = jnp.where(second, -s_high * up_lo, -s_low * up_hi)
    return (as_lower, au_lower, c_lower, as_upper, au_upper, c_upper, slope, b_low, b_high)


def relax(lam_h, tables):
    as_lower, au_lower, c_lower, as_upper, au_upper, c_upper, slope, b_low, b_high = tables
    plus = jnp.maximum(lam_h, 0.0)
    minus = jnp.minimum(lam_h, 0.0)
    lam_u = (plus * au_lower + minus * au_upper).astype(jnp.bfloat16)
    weight_s = plus * as_lower + minus * as_upper
    lam_g = (weight_s * slope).astype(jnp.bfloat16)
    terms = plus * c_lower + minus * c_upper + jnp.maximum(weight_s, 0.0) * b_low + jnp.minimum(weight_s, 0.0) * b_high
    return lam_g, lam_u, jnp.sum(terms, axis=1)


def reference(spec_rows, readout, gate_weight, up_weight, down_weight, gate_lo, gate_width, up_lo, up_width, flags):
    target = jnp.take(readout, spec_rows[:, 0].astype(jnp.int32), axis=0).astype(jnp.float32)
    rival = jnp.take(readout, spec_rows[:, 1].astype(jnp.int32), axis=0).astype(jnp.float32)
    lam = (target - rival).astype(jnp.bfloat16)
    dims = (((1,), (1,)), ((), ()))
    lam_h = lax.dot_general(lam, down_weight, dims, preferred_element_type=jnp.float32)
    tables = unit_tables(gate_lo, gate_width, up_lo, up_width, flags)
    lam_g, lam_u, offsets = relax(lam_h, tables)
    through_gate = lax.dot_general(lam_g, gate_weight, dims, preferred_element_type=jnp.float32)
    through_up = lax.dot_general(lam_u, up_weight, dims, preferred_element_type=jnp.float32)
    input_coeffs = lam.astype(jnp.float32) + through_gate + through_up
    return input_coeffs, offsets
```

```python
import functools

import jax
import jax.numpy as jnp
from jax import lax
from jax.experimental import pallas as pl
from jax.experimental.pallas import tpu as pltpu
from jax.sharding import PartitionSpec as P

MESH = pl.DeviceIdType.MESH
F32 = jnp.float32
BF16 = jnp.bfloat16
NT = (((1,), (1,)), ((), ()))

CHUNKS = 4
OWN = 32
HALF = OWN // 2


def silu(value):
    return value / (1.0 + jnp.exp(-value))


def unit_tables(gate_lo, gate_width, up_lo, up_width, flags):
    gate_hi = gate_lo + gate_width
    up_hi = up_lo + up_width
    middle = 0.5 * (gate_lo + gate_hi)
    valley = jnp.clip(-1.2784645, gate_lo, gate_hi)
    silu_lo = silu(gate_lo)
    silu_hi = silu(gate_hi)
    silu_valley = silu(valley)
    s_low = jnp.minimum(jnp.minimum(silu_lo, silu_hi), silu_valley)
    s_high = jnp.maximum(silu_lo, silu_hi)
    slope = (silu_hi - silu_lo) / gate_width
    rest_a = silu_lo - slope * gate_lo
    rest_b = silu(middle) - slope * middle
    rest_c = silu_valley - slope * valley
    b_low = jnp.minimum(jnp.minimum(rest_a, rest_b), rest_c)
    b_high = jnp.maximum(jnp.maximum(rest_a, rest_b), rest_c)
    second = flags == 1
    as_lower = jnp.where(second, up_hi, up_lo)
    as_upper = jnp.where(second, up_lo, up_hi)
    au = jnp.where(second, s_high, s_low)
    kp = jnp.maximum(as_lower, 0.0) * b_low + jnp.minimum(as_lower, 0.0) * b_high - au * as_lower
    kn = jnp.minimum(as_upper, 0.0) * b_low + jnp.maximum(as_upper, 0.0) * b_high - au * as_upper
    return au, as_lower * slope, as_upper * slope, kp, kn


STEPS = {
    "lam": 0.0,
    "down": 1.5,
    "x1": 7.0,
    "y1": 7.1,
    "x2": 10.0,
    "y2": 10.1,
    "x3": 13.0,
    "y3": 13.1,
    "gx1": 16.0,
    "gy1": 16.1,
    "gx2": 19.0,
    "gy2": 19.1,
    "gx3": 22.0,
    "gy3": 22.1,
    "mm": 24.0,
    "z1": 28.0,
    "z2": 31.0,
    "out": 34.0,
}
STARTS = (0.0, 4.0, 14.0, 25.0)


def kernel(
    spec, readout, gate, up, down, gate_lo, gate_width, up_lo, up_width, flags,
    out, off,
    ro, wp, wn, dn, ds, oh, lam, lams, tab,
    px, py, x1s, x1r, xps, xpr, xqs, xqr, yps, ypr, yqs, yqr, yxs, yxr,
    lx, ly, acc, zps, zpr, zqs, zqr, hs, hr, oacc, obs, obr,
    lsem, ssem, rsem,
):
    hid, wid = lax.axis_index("hid"), lax.axis_index("wid")
    z, xh = hid // 2, hid % 2
    y, a, c = wid // 4, (wid // 2) % 2, wid % 2
    half = dn.shape[0]
    cx, cy = px.shape[-1], py.shape[-1]
    d_own = dn.shape[1]
    rows = CHUNKS * 0 + 8 * OWN
    yu, yd, yo = (y + 1) % 4, (y + 3) % 4, (y + 2) % 4
    zu, zd, zo = (z + 1) % 4, (z + 3) % 4, (z + 2) % 4

    def at(z_, xh_, y_, a_, c_):
        return (z_ * 2 + xh_, (y_ * 2 + a_) * 2 + c_)

    up_y, down_y = at(z, xh, yu, a, c), at(z, xh, yd, a, c)
    other_x = at(z, xh, y, 1 - a, c)
    twin = at(z, xh, y, a, 1 - c)
    up_z, down_z = at(zu, xh, y, a, c), at(zd, xh, y, a, c)
    other_h = at(z, 1 - xh, y, a, c)

    barrier = pltpu.get_barrier_semaphore()
    for device in (up_y, down_y, other_x, twin, up_z, down_z, other_h):
        pl.semaphore_signal(barrier, inc=1, device_id=device, device_id_type=MESH)

    load_ro = pltpu.make_async_copy(readout, ro, lsem.at[0])
    load_ro.start()
    my_half = pl.multiple_of(c * half, half)
    its_half = pl.multiple_of((1 - c) * half, half)
    load_dx = pltpu.make_async_copy(down.at[pl.ds(my_half, cx)], dn.at[pl.ds(0, cx)], lsem.at[1])
    load_dy = pltpu.make_async_copy(
        down.at[pl.ds(pl.multiple_of(my_half + cx, 256), cy)], dn.at[pl.ds(cx, cy)], lsem.at[2]
    )
    load_dx.start()
    load_dy.start()
    load_up = pltpu.make_async_copy(up, wp, lsem.at[3])
    load_gate = pltpu.make_async_copy(gate, wn, lsem.at[4])
    load_up.start()
    load_gate.start()

    copies = {}
    index = {}

    def send(name, r, src, dst, device):
        k = index.setdefault(name, len(index))
        copy = pltpu.make_async_remote_copy(
            src_ref=src, dst_ref=dst, send_sem=ssem.at[k, r], recv_sem=rsem.at[k, r],
            device_id=device, device_id_type=MESH,
        )
        copy.start()
        copies[name, r] = copy

    def arrive(name, r):
        copies[name, r].wait_recv()

    for k, table in enumerate(
        unit_tables(gate_lo[...], gate_width[...], up_lo[...], up_width[...], flags[...])
    ):
        tab[k, 0 : table.shape[0], :] = table

    def lam_rows(r):
        def group(g, carry):
            a_, y_, co = g // 8, (g // 2) % 4, g % 2
            start = pl.multiple_of((y_ * 2 + a_) * 128 + co * 64 + r * 16, 16)
            pair = spec[pl.ds(start, 16), :]
            classes = lax.broadcasted_iota(jnp.int32, (16, ro.shape[0]), 1)
            picked = jnp.where(classes == pair[:, 0:1], 1.0, 0.0) - jnp.where(classes == pair[:, 1:2], 1.0, 0.0)
            oh[pl.ds(pl.multiple_of(g * 16, 16), 16), :] = picked.astype(BF16)
            return carry

        lax.fori_loop(0, 16, group, 0)
        lam[r] = jnp.dot(oh[...], ro[...], preferred_element_type=F32).astype(BF16)

    def tree_first(stage, get, u, d, o):
        lead = (slice(None),) * (len(stage.shape) - 3)
        stage[(0, *lead, slice(0, HALF))] = get(o, 0).astype(stage.dtype)
        stage[(0, *lead, slice(HALF, OWN))] = get(u, 1).astype(stage.dtype)
        stage[(1, *lead, slice(0, HALF))] = get(d, 0).astype(stage.dtype)
        stage[(1, *lead, slice(HALF, OWN))] = get(o, 1).astype(stage.dtype)

    def tree_second(stage, came, get, u, d):
        lead = (slice(None),) * (len(came.shape) - 3)
        stage[0] = (get(u, 0) + came[(0, *lead, slice(0, HALF))].astype(F32)).astype(stage.dtype)
        stage[1] = (get(d, 1) + came[(1, *lead, slice(HALF, OWN))].astype(F32)).astype(stage.dtype)

    def tree_last(came, second, get, own):
        lead = (slice(None),) * (len(came.shape) - 3)
        low = get(own, 0) + came[(1, *lead, slice(0, HALF))].astype(F32) + second[0].astype(F32)
        high = get(own, 1) + came[(0, *lead, slice(HALF, OWN))].astype(F32) + second[1].astype(F32)
        return low, high

    def halves(h):
        return slice(h * HALF, (h + 1) * HALF)

    def get_x(r):
        return lambda y_, h: px[r, a * 4 + y_, halves(h)]

    def get_y(r):
        return lambda y_, h: py[r, :, y_, halves(h)]

    def get_z(r):
        return lambda z_, h: acc[r, :, z_, halves(h)]

    def constant_terms(r, h, value, first):
        blocks = value.shape[-1] // 128
        total = jnp.zeros((HALF, 128), F32)
        for j in range(blocks):
            row = c * (half // 128) + first + j
            part = value[:, j * 128 : (j + 1) * 128]
            total = total + jnp.maximum(part, 0.0) * tab[3, pl.ds(row, 1), :]
            total = total + jnp.minimum(part, 0.0) * tab[4, pl.ds(row, 1), :]
        if first == 0:
            oacc[h, r] = total
        else:
            oacc[h, r] += total

    def step_lam(r):
        if r == 0:
            load_ro.wait()
        lam_rows(r)
        if r == 0:
            pl.semaphore_wait(barrier, 7)
            send("lam", r, lam.at[r], lams.at[r], twin)
            send("dx", 0, down.at[pl.ds(its_half, cx)], ds.at[pl.ds(0, cx)], twin)
            send("dy", 0, down.at[pl.ds(pl.multiple_of(its_half + cx, 256), cy)], ds.at[pl.ds(cx, cy)], twin)
        else:
            send("lam", r, lam.at[r], lams.at[r], twin)

    def times_down(r, first, count, target):
        def block(n, carry):
            units = pl.ds(pl.multiple_of(first + n * 256, 256), 256)
            part = lax.dot_general(lam[r], dn[units, :], NT, preferred_element_type=F32)
            part = part + lax.dot_general(lams[r], ds[units, :], NT, preferred_element_type=F32)
            target(pl.ds(pl.multiple_of(n * 256, 256), 256), part)
            return carry

        lax.fori_loop(0, count // 256, block, 0)

    def step_down(r):
        arrive("lam", r)
        if r == 0:
            load_dx.wait()
            arrive("dx", 0)

        def to_x(columns, part):
            px[r, :, :, columns] = part.reshape(8, OWN, 256)

        def to_y(columns, part):
            py[r, :, :, :, columns] = part.reshape(2, 4, OWN, 256)

        times_down(r, 0, cx, to_x)
        x1s[r] = px[r, pl.ds((1 - a) * 4, 4)].astype(BF16)
        send("x1", r, x1s.at[r], x1r.at[r], other_x)
        if r == 0:
            load_dy.wait()
            arrive("dy", 0)
        times_down(r, cx, cy, to_y)
        tree_first(yps.at[r], get_y(r), yu, yd, yo)
        send("yu1", r, yps.at[r, 0], ypr.at[r, 0], up_y)
        send("yd1", r, yps.at[r, 1], ypr.at[r, 1], down_y)

    def step_x1(r):
        arrive("x1", r)
        mine = pl.ds(a * 4, 4)
        px[r, mine] += x1r[r].astype(F32)
        tree_first(xps.at[r], get_x(r), yu, yd, yo)
        send("xu1", r, xps.at[r, 0], xpr.at[r, 0], up_y)
        send("xd1", r, xps.at[r, 1], xpr.at[r, 1], down_y)

    def step_y1(r):
        arrive("yu1", r)
        arrive("yd1", r)
        tree_second(yqs.at[r], ypr.at[r], get_y(r), yu, yd)
        send("yu2", r, yqs.at[r, 0], yqr.at[r, 0], up_y)
        send("yd2", r, yqs.at[r, 1], yqr.at[r, 1], down_y)

    def step_x2(r):
        arrive("xu1", r)
        arrive("xd1", r)
        tree_second(xqs.at[r], xpr.at[r], get_x(r), yu, yd)
        send("xu2", r, xqs.at[r, 0], xqr.at[r, 0], up_y)
        send("xd2", r, xqs.at[r, 1], xqr.at[r, 1], down_y)

    def step_y2(r):
        arrive("yu2", r)
        arrive("yd2", r)
        low, high = tree_last(ypr.at[r], yqr.at[r], get_y(r), y)
        py[r, :, y, halves(0)] = low
        py[r, :, y, halves(1)] = high
        yxs[r] = py[r, 1 - a, y].astype(BF16)
        send("yx", r, yxs.at[r], yxr.at[r], other_x)

    def step_x3(r):
        arrive("xu2", r)
        arrive("xd2", r)
        for h, value in enumerate(tree_last(xpr.at[r], xqr.at[r], get_x(r), y)):
            lx[r, c, a, y, halves(h)] = value.astype(BF16)
            constant_terms(r, h, value, 0)
        block = lx.at[r, c, a, y]
        send("gxu1", r, block, block, up_y)
        send("gxd1", r, block, block, down_y)
        send("gxx0", r, block, block, other_x)

    def step_y3(r):
        arrive("yx", r)
        for h in range(2):
            value = py[r, a, y, halves(h)] + yxr[r, halves(h)].astype(F32)
            ly[r, c, a, y, halves(h)] = value.astype(BF16)
            constant_terms(r, h, value, cx // 128)
        block = ly.at[r, c, a, y]
        send("gyx", r, block, block, other_x)
        send("gyu1", r, block, block, up_y)
        send("gyd1", r, block, block, down_y)

    def step_gx1(r):
        arrive("gxu1", r)
        arrive("gxd1", r)
        below = lx.at[r, c, a, yd, halves(0)]
        above = lx.at[r, c, a, yu, halves(1)]
        send("gxu2", r, below, below, up_y)
        send("gxd2", r, above, above, down_y)
        for name, y_ in (("gxx1", yu), ("gxx2", yd)):
            block = lx.at[r, c, a, y_]
            send(name, r, block, block, other_x)

    def step_gy1(r):
        arrive("gyx", r)
        block = ly.at[r, c, 1 - a, y]
        send("gyu1b", r, block, block, up_y)
        send("gyd1b", r, block, block, down_y)

    def step_gx2(r):
        arrive("gxu2", r)
        arrive("gxd2", r)
        block = lx.at[r, c, a, yo]
        send("gxx3", r, block, block, other_x)
        block = lx.at[r, c, a]
        send("tx0", r, block, block, twin)

    def step_gy2(r):
        for name in ("gyu1", "gyd1", "gyu1b", "gyd1b"):
            arrive(name, r)
        below = ly.at[r, c, :, yd, halves(0)]
        above = ly.at[r, c, :, yu, halves(1)]
        send("gyu2", r, below, below, up_y)
        send("gyd2", r, above, above, down_y)

    def step_gx3(r):
        for k in range(4):
            arrive("gxx%d" % k, r)
        block = lx.at[r, c, 1 - a]
        send("tx1", r, block, block, twin)

    def step_gy3(r):
        arrive("gyu2", r)
        arrive("gyd2", r)
        block = ly.at[r, c]
        send("ty", r, block, block, twin)

    def times_weights(r, cc, add):
        base = cc * half
        columns_x = pl.ds(pl.multiple_of(base, 256), cx)
        columns_y = pl.ds(pl.multiple_of(base + cx, 256), cy)

        def block(n, carry):
            units = pl.ds(pl.multiple_of(n * 256, 256), 256)
            total = None
            for ref, columns in ((lx, columns_x), (ly, columns_y)):
                value = ref[r, cc].reshape(rows, columns.size)
                for part, weight in ((jnp.maximum(value, 0), wp), (jnp.minimum(value, 0), wn)):
                    term = lax.dot_general(part, weight[units, columns], NT, preferred_element_type=F32)
                    total = term if total is None else total + term
            total = total.reshape(2, 4, OWN, 256)
            if add:
                acc[r, :, :, :, units] += total
            else:
                acc[r, :, :, :, units] = total
            return carry

        lax.fori_loop(0, d_own // 256, block, 0)

    def step_mm(r):
        times_weights(r, c, False)
        arrive("tx0", r)
        arrive("tx1", r)
        arrive("ty", r)
        times_weights(r, 1 - c, True)
        tree_first(zps.at[r], get_z(r), zu, zd, zo)
        send("zu1", r, zps.at[r, 0], zpr.at[r, 0], up_z)
        send("zd1", r, zps.at[r, 1], zpr.at[r, 1], down_z)

    def step_z1(r):
        arrive("zu1", r)
        arrive("zd1", r)
        tree_second(zqs.at[r], zpr.at[r], get_z(r), zu, zd)
        send("zu2", r, zqs.at[r, 0], zqr.at[r, 0], up_z)
        send("zd2", r, zqs.at[r, 1], zqr.at[r, 1], down_z)

    def step_z2(r):
        arrive("zu2", r)
        arrive("zd2", r)
        low, high = tree_last(zpr.at[r], zqr.at[r], get_z(r), z)
        acc[r, :, z, halves(0)] = low
        acc[r, :, z, halves(1)] = high
        hs[r] = acc[r, 1 - xh, z]
        send("h", r, hs.at[r], hr.at[r], other_h)

    def step_out(r):
        arrive("h", r)
        first = (xh * 4 + z) * OWN
        for h in range(2):
            own = lam[r, pl.ds(pl.multiple_of(first + h * HALF, HALF), HALF), :].astype(F32)
            out[h * 64 + r * HALF : h * 64 + (r + 1) * HALF, :] = own + acc[r, xh, z, halves(h)] + hr[r, halves(h)]

    def weights(k):
        if k == 0:
            load_up.wait()
            load_gate.wait()

        def block(j, carry):
            columns = pl.ds(pl.multiple_of(j * 128, 128), 128)
            scaled = wp[:, columns].astype(F32) * tab[0, pl.ds(j, 1), :]
            gates = wn[:, columns].astype(F32)
            wp[:, columns] = (scaled + gates * tab[1, pl.ds(j, 1), :]).astype(BF16)
            wn[:, columns] = (scaled + gates * tab[2, pl.ds(j, 1), :]).astype(BF16)
            return carry

        count = wp.shape[1] // 128 // 2
        lax.fori_loop(k * count, (k + 1) * count, block, 0)

    partners = (
        twin,
        at(z + 1 - 2 * (z % 2), xh, y, a, c),
        at(3 - z, xh, y, a, c),
        other_h,
    )

    def offset_start():
        obs[0] = jnp.broadcast_to(jnp.sum(oacc[...].reshape(128, 128).T, axis=0, keepdims=True), (8, 128))
        send("o", 0, obs.at[0], obr.at[0], partners[0])

    def offset_step(k):
        arrive("o", k - 1)
        if k < 4:
            obs[k] = obs[k - 1] + obr[k - 1]
            send("o", k, obs.at[k], obr.at[k], partners[k])
        else:
            total = obs[k - 1] + obr[k - 1]
            off[...] = jnp.where(c == 0, total[0:1, 0:64], total[0:1, 64:128])

    table = dict(
        lam=step_lam, down=step_down, x1=step_x1, y1=step_y1, x2=step_x2, y2=step_y2, x3=step_x3, y3=step_y3,
        gx1=step_gx1, gy1=step_gy1, gx2=step_gx2, gy2=step_gy2, gx3=step_gx3, gy3=step_gy3,
        mm=step_mm, z1=step_z1, z2=step_z2, out=step_out,
    )
    plan = [
        (start + when, functools.partial(table[name], r))
        for r, start in enumerate(STARTS)
        for name, when in STEPS.items()
    ]
    plan.append((STARTS[1] + 2.0, functools.partial(weights, 0)))
    plan.append((STARTS[1] + 6.05, functools.partial(weights, 1)))
    last = STARTS[-1]
    plan.append((last + 13.2, offset_start))
    for k, when in ((1, 19.2), (2, 22.2), (3, 28.2), (4, 31.2)):
        plan.append((last + when, functools.partial(offset_step, k)))
    for _, step in sorted(plan, key=lambda item: item[0]):
        step()
    for copy in copies.values():
        copy.wait_send()


def per_device(
    spec_rows, readout, gate_weight, up_weight, down_weight, gate_lo, gate_width, up_lo, up_width, flags
):
    d_own = readout.shape[1]
    units = down_weight.shape[0]
    half = units // 2
    cx = 768
    cy = half - cx
    rows = 8 * OWN
    r = CHUNKS
    lanes = [value.reshape(units // 128, 128) for value in (gate_lo, gate_width, up_lo, up_width, flags)]
    vm = pltpu.VMEM
    scratch = [
        vm((readout.shape[0], d_own), BF16),
        vm((d_own, units), BF16),
        vm((d_own, units), BF16),
        vm((half, d_own), BF16),
        vm((half, d_own), BF16),
        vm((rows, readout.shape[0]), BF16),
        vm((r, rows, d_own), BF16),
        vm((r, rows, d_own), BF16),
        vm((5, 32, 128), F32),
        vm((r, 8, OWN, cx), F32),
        vm((r, 2, 4, OWN, cy), F32),
        vm((r, 4, OWN, cx), BF16),
        vm((r, 4, OWN, cx), BF16),
        vm((r, 2, OWN, cx), BF16),
        vm((r, 2, OWN, cx), BF16),
        vm((r, 2, HALF, cx), BF16),
        vm((r, 2, HALF, cx), BF16),
        vm((r, 2, 2, OWN, cy), BF16),
        vm((r, 2, 2, OWN, cy), BF16),
        vm((r, 2, 2, HALF, cy), BF16),
        vm((r, 2, 2, HALF, cy), BF16),
        vm((r, OWN, cy), BF16),
        vm((r, OWN, cy), BF16),
        vm((r, 2, 2, 4, OWN, cx), BF16),
        vm((r, 2, 2, 4, OWN, cy), BF16),
        vm((r, 2, 4, OWN, d_own), F32),
        vm((r, 2, 2, OWN, d_own), F32),
        vm((r, 2, 2, OWN, d_own), F32),
        vm((r, 2, 2, HALF, d_own), F32),
        vm((r, 2, 2, HALF, d_own), F32),
        vm((r, OWN, d_own), F32),
        vm((r, OWN, d_own), F32),
        vm((2, r, HALF, 128), F32),
        vm((4, 8, 128), F32),
        vm((4, 8, 128), F32),
        pltpu.SemaphoreType.DMA((5,)),
        pltpu.SemaphoreType.DMA((40, r)),
        pltpu.SemaphoreType.DMA((40, r)),
    ]
    held = pl.BlockSpec(memory_space=pltpu.VMEM)
    far = pl.BlockSpec(memory_space=pl.ANY)
    coeffs, offsets = pl.pallas_call(
        kernel,
        name="bound_pass",
        out_shape=(
            jax.ShapeDtypeStruct((spec_rows.shape[0] // 8, d_own), F32),
            jax.ShapeDtypeStruct((1, 64), F32),
        ),
        in_specs=[held, far, far, far, far, held, held, held, held, held],
        out_specs=(held, held),
        scratch_shapes=scratch,
        compiler_params=pltpu.CompilerParams(
            collective_id=0, has_side_effects=True, vmem_limit_bytes=60 * 1024 * 1024
        ),
    )(spec_rows, readout, gate_weight, up_weight, down_weight, *lanes)
    return coeffs, offsets.reshape(64)


def solution(mesh):
    placed = (
        P(),
        P(None, "wid"),
        P("wid", "hid"),
        P("wid", "hid"),
        P("hid", "wid"),
        P("hid"),
        P("hid"),
        P("hid"),
        P("hid"),
        P("hid"),
    )
    return jax.shard_map(
        per_device,
        mesh=mesh,
        in_specs=placed,
        out_specs=(P("hid", "wid"), P("wid")),
        check_vma=False,
    )
```

```python
import jax
import jax.numpy as jnp
from jax import lax
from jax.experimental import pallas as pl
from jax.experimental.pallas import tpu as pltpu
from jax.sharding import PartitionSpec as P

MESH = pl.DeviceIdType.MESH
F32 = jnp.float32
BF16 = jnp.bfloat16
NT = (((1,), (1,)), ((), ()))

CHUNKS = 4
OWN = 32
HALF = OWN // 2


def silu(value):
    return value / (1.0 + jnp.exp(-value))


def unit_tables(gate_lo, gate_width, up_lo, up_width, flags):
    gate_hi = gate_lo + gate_width
    up_hi = up_lo + up_width
    middle = 0.5 * (gate_lo + gate_hi)
    valley = jnp.clip(-1.2784645, gate_lo, gate_hi)
    silu_lo = silu(gate_lo)
    silu_hi = silu(gate_hi)
    silu_valley = silu(valley)
    s_low = jnp.minimum(jnp.minimum(silu_lo, silu_hi), silu_valley)
    s_high = jnp.maximum(silu_lo, silu_hi)
    slope = (silu_hi - silu_lo) / gate_width
    rest_a = silu_lo - slope * gate_lo
    rest_b = silu(middle) - slope * middle
    rest_c = silu_valley - slope * valley
    b_low = jnp.minimum(jnp.minimum(rest_a, rest_b), rest_c)
    b_high = jnp.maximum(jnp.maximum(rest_a, rest_b), rest_c)
    second = flags == 1
    as_lower = jnp.where(second, up_hi, up_lo)
    as_upper = jnp.where(second, up_lo, up_hi)
    au = jnp.where(second, s_high, s_low)
    kp = jnp.maximum(as_lower, 0.0) * b_low + jnp.minimum(as_lower, 0.0) * b_high - au * as_lower
    kn = jnp.minimum(as_upper, 0.0) * b_low + jnp.maximum(as_upper, 0.0) * b_high - au * as_upper
    return au, as_lower * slope, as_upper * slope, kp, kn


PLAN = (
    ("lam", 0), ("lam", 1), ("downx", 0), ("downy", 0), ("downx", 1), ("downy", 1), ("lam", 2), ("y1", 0),
    ("x1", 0), ("downx", 2), ("y1", 1), ("downy", 2), ("y2", 0), ("x2", 0), ("x1", 1), ("x3", 0), ("y2", 1),
    ("x2", 1), ("y3", 0), ("lam", 3), ("x1", 2), ("gx1", 0), ("y3", 1), ("gy1", 0), ("w", 0), ("x3", 1),
    ("gx2", 0), ("downx", 3), ("x2", 2), ("gy1", 1), ("gy2", 0), ("gx3", 0), ("y1", 2), ("x3", 2), ("gy3", 0),
    ("gx1", 1), ("gy2", 1), ("downy", 3), ("y2", 2), ("w", 1), ("x1", 3), ("gx2", 1), ("mma", 0), ("y3", 2),
    ("gx1", 2), ("gy3", 1), ("mm", 0), ("gx3", 1), ("y1", 3), ("mma", 1), ("x2", 3), ("gy1", 2), ("y2", 3),
    ("x3", 3), ("mm", 1), ("gx2", 2), ("gy2", 2), ("y3", 3), ("o", 0), ("gx3", 2), ("gx1", 3), ("o", 1),
    ("gy3", 2), ("gy1", 3), ("mma", 2), ("mm", 2), ("z1", 1), ("gy3", 3), ("z1", 0), ("gx3", 3), ("o", 2),
    ("mma", 3), ("mm", 3), ("o", 3), ("z1", 2), ("out", 0), ("out", 1), ("o", 4), ("out", 3), ("out", 2),
)
LAST = CHUNKS - 1


def kernel(
    spec, readout, gate, up, down, gate_lo, gate_width, up_lo, up_width, flags,
    out, off,
    ro, wp, wn, dn, pairs, oh, lam, tab,
    px, py, x1s, x1r, xps, xpr, xqs, xqr, yps, ypr, yqs, yqr, yxs, yxr,
    lx, ly, acc, zr, hs, hr, ends, endr, oacc, obs, obr,
    lsem, ssem, rsem,
):
    hid, wid = lax.axis_index("hid"), lax.axis_index("wid")
    z, xh = hid // 2, hid % 2
    y, a, c = wid // 4, (wid // 2) % 2, wid % 2
    half = dn.shape[0]
    cx, cy = px.shape[-1], py.shape[-1]
    d_own = ro.shape[1]
    rows = 8 * OWN
    mine, its = pl.ds(0, d_own), pl.ds(d_own, d_own)
    yu, yd, yo = (y + 1) % 4, (y + 3) % 4, (y + 2) % 4
    zu, zd, zo = (z + 1) % 4, (z + 3) % 4, (z + 2) % 4

    def at(z_, xh_, y_, a_, c_):
        return (z_ * 2 + xh_, (y_ * 2 + a_) * 2 + c_)

    up_y, down_y = at(z, xh, yu, a, c), at(z, xh, yd, a, c)
    other_x = at(z, xh, y, 1 - a, c)
    twin = at(z, xh, y, a, 1 - c)
    over_y = at(z, xh, yo, a, c)
    by_z = {(s, f): at((z + s) % 4, (xh + f) % 2, y, a, c) for s in range(4) for f in range(2) if s or f}
    other_h = by_z[0, 1]

    barrier = pltpu.get_barrier_semaphore()
    for device in (up_y, down_y, over_y, other_x, twin, *by_z.values()):
        pl.semaphore_signal(barrier, inc=1, device_id=device, device_id_type=MESH)

    load_ro = pltpu.make_async_copy(readout, ro, lsem.at[0])
    load_ro.start()
    my_half = pl.multiple_of(c * half, half)
    its_half = pl.multiple_of((1 - c) * half, half)
    load_dx = pltpu.make_async_copy(down.at[pl.ds(my_half, cx)], dn.at[pl.ds(0, cx), mine], lsem.at[1])
    load_dy = pltpu.make_async_copy(
        down.at[pl.ds(pl.multiple_of(my_half + cx, 256), cy)], dn.at[pl.ds(cx, cy), mine], lsem.at[2]
    )
    load_dx.start()
    load_dy.start()
    load_up = pltpu.make_async_copy(up, wp, lsem.at[3])
    load_gate = pltpu.make_async_copy(gate, wn, lsem.at[4])
    load_up.start()
    load_gate.start()

    copies = {}
    index = {}

    def send(name, r, src, dst, device):
        k = index.setdefault(name, len(index))
        copy = pltpu.make_async_remote_copy(
            src_ref=src, dst_ref=dst, send_sem=ssem.at[k, r], recv_sem=rsem.at[k, r],
            device_id=device, device_id_type=MESH,
        )
        copy.start()
        copies[name, r] = copy

    def arrive(name, r):
        copies[name, r].wait_recv()

    for k, table in enumerate(
        unit_tables(gate_lo[...], gate_width[...], up_lo[...], up_width[...], flags[...])
    ):
        tab[k, 0 : table.shape[0], :] = table

    tall = jnp.concatenate([spec[...].astype(F32), jnp.zeros((6, spec.shape[1]), F32)], axis=0)
    pairs[...] = tall.T
    oacc[...] = jnp.zeros_like(oacc)

    def lam_rows(r):
        def group(g, carry):
            a_, y_, co = g // 8, (g // 2) % 4, g % 2
            start = pl.multiple_of((y_ * 2 + a_) * 128 + co * 64 + r * 16, 16)
            pair = pairs[pl.ds(start, 16), :].astype(jnp.int32)
            classes = lax.broadcasted_iota(jnp.int32, (16, ro.shape[0]), 1)
            picked = jnp.where(classes == pair[:, 0:1], 1.0, 0.0) - jnp.where(classes == pair[:, 1:2], 1.0, 0.0)
            oh[pl.ds(pl.multiple_of(g * 16, 16), 16), :] = picked.astype(BF16)
            return carry

        lax.fori_loop(0, 16, group, 0)
        lam[r, :, 0:d_own] = jnp.dot(oh[...], ro[...], preferred_element_type=F32).astype(BF16)

    def tree_first(stage, get, u, d, o):
        lead = (slice(None),) * (len(stage.shape) - 3)
        stage[(0, *lead, slice(0, HALF))] = get(o, 0).astype(stage.dtype)
        stage[(0, *lead, slice(HALF, OWN))] = get(u, 1).astype(stage.dtype)
        stage[(1, *lead, slice(0, HALF))] = get(d, 0).astype(stage.dtype)
        stage[(1, *lead, slice(HALF, OWN))] = get(o, 1).astype(stage.dtype)

    def tree_second(stage, came, get, u, d):
        lead = (slice(None),) * (len(came.shape) - 3)
        stage[0] = (get(u, 0) + came[(0, *lead, slice(0, HALF))].astype(F32)).astype(stage.dtype)
        stage[1] = (get(d, 1) + came[(1, *lead, slice(HALF, OWN))].astype(F32)).astype(stage.dtype)

    def tree_last(came, second, get, own):
        lead = (slice(None),) * (len(came.shape) - 3)
        low = get(own, 0) + came[(1, *lead, slice(0, HALF))].astype(F32) + second[0].astype(F32)
        high = get(own, 1) + came[(0, *lead, slice(HALF, OWN))].astype(F32) + second[1].astype(F32)
        return low, high

    def halves(h):
        return slice(h * HALF, (h + 1) * HALF)

    def get_x(r):
        return lambda y_, h: px[r, a * 4 + y_, halves(h)]

    def get_y(r):
        return lambda y_, h: py[r, :, y_, halves(h)]

    def get_z(r):
        return lambda z_, h: acc[r, :, z_, halves(h)]

    def constant_terms(r, h, value, first):
        blocks = value.shape[-1] // 128
        total = jnp.zeros((HALF, 128), F32)
        for j in range(blocks):
            row = c * (half // 128) + first + j
            part = value[:, j * 128 : (j + 1) * 128]
            total = total + jnp.maximum(part, 0.0) * tab[3, pl.ds(row, 1), :]
            total = total + jnp.minimum(part, 0.0) * tab[4, pl.ds(row, 1), :]
        oacc[h, r] += total

    def step_lam(r):
        if r == 0:
            load_ro.wait()
        lam_rows(r)
        if r == 0:
            pl.semaphore_wait(barrier, 5 + len(by_z))
        send("lam", r, lam.at[r, :, mine], lam.at[r, :, its], twin)
        if r == 0:
            send("dx", 0, down.at[pl.ds(its_half, cx)], dn.at[pl.ds(0, cx), its], twin)
            later = pl.ds(pl.multiple_of(its_half + cx, 256), cy)
            send("dy", 0, down.at[later], dn.at[pl.ds(cx, cy), its], twin)

    def times_down(r, units):
        return lax.dot_general(lam[r], dn[units, :], NT, preferred_element_type=F32)

    def step_downx(r):
        if r == 0:
            load_dx.wait()
            arrive("dx", 0)
        arrive("lam", r)
        for n in range(cx // 256):
            columns = slice(n * 256, (n + 1) * 256)
            px[r, :, :, columns] = times_down(r, columns).reshape(8, OWN, 256)
        x1s[r] = px[r, pl.ds((1 - a) * 4, 4)].astype(BF16)
        send("x1", r, x1s.at[r], x1r.at[r], other_x)

    def step_downy(r):
        if r == 0:
            load_dy.wait()
            arrive("dy", 0)
        for n in range(cy // 256):
            columns = slice(n * 256, (n + 1) * 256)
            units = slice(cx + n * 256, cx + (n + 1) * 256)
            py[r, :, :, :, columns] = times_down(r, units).reshape(2, 4, OWN, 256)
        tree_first(yps.at[r], get_y(r), yu, yd, yo)
        send("yu1", r, yps.at[r, 0], ypr.at[r, 0], up_y)
        send("yd1", r, yps.at[r, 1], ypr.at[r, 1], down_y)

    def step_x1(r):
        arrive("x1", r)
        own = pl.ds(a * 4, 4)
        px[r, own] += x1r[r].astype(F32)
        tree_first(xps.at[r], get_x(r), yu, yd, yo)
        send("xu1", r, xps.at[r, 0], xpr.at[r, 0], up_y)
        send("xd1", r, xps.at[r, 1], xpr.at[r, 1], down_y)

    def step_y1(r):
        arrive("yu1", r)
        arrive("yd1", r)
        tree_second(yqs.at[r], ypr.at[r], get_y(r), yu, yd)
        send("yu2", r, yqs.at[r, 0], yqr.at[r, 0], up_y)
        send("yd2", r, yqs.at[r, 1], yqr.at[r, 1], down_y)

    def step_x2(r):
        arrive("xu1", r)
        arrive("xd1", r)
        tree_second(xqs.at[r], xpr.at[r], get_x(r), yu, yd)
        send("xu2", r, xqs.at[r, 0], xqr.at[r, 0], up_y)
        send("xd2", r, xqs.at[r, 1], xqr.at[r, 1], down_y)

    def step_y2(r):
        arrive("yu2", r)
        arrive("yd2", r)
        low, high = tree_last(ypr.at[r], yqr.at[r], get_y(r), y)
        py[r, :, y, halves(0)] = low
        py[r, :, y, halves(1)] = high
        yxs[r] = py[r, 1 - a, y].astype(BF16)
        send("yx", r, yxs.at[r], yxr.at[r], other_x)

    def step_x3(r):
        arrive("xu2", r)
        arrive("xd2", r)
        for h, value in enumerate(tree_last(xpr.at[r], xqr.at[r], get_x(r), y)):
            lx[r, c, a, y, halves(h)] = value.astype(BF16)
            constant_terms(r, h, value, 0)
        block = lx.at[r, c, a, y]
        send("gxu1", r, block, block, up_y)
        send("gxd1", r, block, block, down_y)
        send("gxx0", r, block, block, other_x)
        if r == LAST:
            send("gxo", r, block, block, over_y)

    def step_y3(r):
        arrive("yx", r)
        for h in range(2):
            value = py[r, a, y, halves(h)] + yxr[r, halves(h)].astype(F32)
            ly[r, c, a, y, halves(h)] = value.astype(BF16)
            constant_terms(r, h, value, cx // 128)
        block = ly.at[r, c, a, y]
        send("gyx", r, block, block, other_x)
        send("gyu1", r, block, block, up_y)
        send("gyd1", r, block, block, down_y)
        if r == LAST:
            send("gyo", r, block, block, over_y)

    def step_gx1(r):
        arrive("gxu1", r)
        arrive("gxd1", r)
        if r == LAST:
            arrive("gxo", r)
            for name, y_ in (("gxx1", yu), ("gxx2", yd), ("gxx3", yo)):
                block = lx.at[r, c, a, y_]
                send(name, r, block, block, other_x)
            block = lx.at[r, c, a]
            send("tx0", r, block, block, twin)
            return
        below = lx.at[r, c, a, yd, halves(0)]
        above = lx.at[r, c, a, yu, halves(1)]
        send("gxu2", r, below, below, up_y)
        send("gxd2", r, above, above, down_y)
        for name, y_ in (("gxx1", yu), ("gxx2", yd)):
            block = lx.at[r, c, a, y_]
            send(name, r, block, block, other_x)

    def step_gy1(r):
        arrive("gyx", r)
        block = ly.at[r, c, 1 - a, y]
        send("gyu1b", r, block, block, up_y)
        send("gyd1b", r, block, block, down_y)
        if r == LAST:
            send("gyob", r, block, block, over_y)

    def step_gx2(r):
        arrive("gxu2", r)
        arrive("gxd2", r)
        block = lx.at[r, c, a, yo]
        send("gxx3", r, block, block, other_x)
        block = lx.at[r, c, a]
        send("tx0", r, block, block, twin)

    def step_gy2(r):
        for name in ("gyu1", "gyd1", "gyu1b", "gyd1b"):
            arrive(name, r)
        below = ly.at[r, c, :, yd, halves(0)]
        above = ly.at[r, c, :, yu, halves(1)]
        send("gyu2", r, below, below, up_y)
        send("gyd2", r, above, above, down_y)

    def step_gx3(r):
        for k in range(4):
            arrive("gxx%d" % k, r)
        block = lx.at[r, c, 1 - a]
        send("tx1", r, block, block, twin)

    def step_gy3(r):
        if r == LAST:
            for name in ("gyu1", "gyd1", "gyu1b", "gyd1b", "gyo", "gyob"):
                arrive(name, r)
        else:
            arrive("gyu2", r)
            arrive("gyd2", r)
        block = ly.at[r, c]
        send("ty", r, block, block, twin)

    def times_weights(r, cc, add):
        base = cc * half
        columns_x = pl.ds(pl.multiple_of(base, 256), cx)
        columns_y = pl.ds(pl.multiple_of(base + cx, 256), cy)

        def block(n, carry):
            units = pl.ds(pl.multiple_of(n * 256, 256), 256)
            total = None
            for ref, columns in ((lx, columns_x), (ly, columns_y)):
                value = ref[r, cc].reshape(rows, columns.size)
                for part, weight in ((jnp.maximum(value, 0), wp), (jnp.minimum(value, 0), wn)):
                    term = lax.dot_general(part, weight[units, columns], NT, preferred_element_type=F32)
                    total = term if total is None else total + term
            total = total.reshape(2, 4, OWN, 256)
            if add:
                acc[r, :, :, :, units] += total
            else:
                acc[r, :, :, :, units] = total
            return carry

        lax.fori_loop(0, d_own // 256, block, 0)

    def step_mma(r):
        times_weights(r, c, False)

    def step_mm(r):
        arrive("tx0", r)
        arrive("tx1", r)
        arrive("ty", r)
        times_weights(r, 1 - c, True)
        if r == LAST:
            ends[...] = acc[r].astype(BF16)
            for (s, f), device in by_z.items():
                send("e%d%d" % (s, f), r, ends.at[(xh + f) % 2, (z + s) % 4], endr.at[s * 2 + f], device)
        else:
            for s, z_ in ((1, zu), (3, zd), (2, zo)):
                send("z%d" % s, r, acc.at[r, :, z_], zr.at[r, s - 1], by_z[s, 0])

    def step_z1(r):
        for s in (1, 3, 2):
            arrive("z%d" % s, r)
        hs[r] = (acc[r, 1 - xh, z] + zr[r, 0, 1 - xh]) + (zr[r, 1, 1 - xh] + zr[r, 2, 1 - xh])
        send("h", r, hs.at[r], hr.at[r], other_h)

    def step_out(r):
        first = pl.multiple_of((xh * 4 + z) * OWN, OWN)
        total = lam[r, pl.ds(first, OWN), 0:d_own].astype(F32) + acc[r, xh, z]
        if r == LAST:
            for s, f in by_z:
                arrive("e%d%d" % (s, f), r)
                total = total + endr[s * 2 + f].astype(F32)
        else:
            total = total + (zr[r, 0, xh] + zr[r, 1, xh] + zr[r, 2, xh])
            arrive("h", r)
            total = total + hr[r]
        for h in range(2):
            out[h * 64 + r * HALF : h * 64 + (r + 1) * HALF, :] = total[halves(h)]

    def weights(k):
        if k == 0:
            load_up.wait()
            load_gate.wait()

        def block(j, carry):
            columns = pl.ds(pl.multiple_of(j * 128, 128), 128)
            scaled = wp[:, columns].astype(F32) * tab[0, pl.ds(j, 1), :]
            gates = wn[:, columns].astype(F32)
            wp[:, columns] = (scaled + gates * tab[1, pl.ds(j, 1), :]).astype(BF16)
            wn[:, columns] = (scaled + gates * tab[2, pl.ds(j, 1), :]).astype(BF16)
            return carry

        count = wp.shape[1] // 128 // 2
        lax.fori_loop(k * count, (k + 1) * count, block, 0)

    partners = (
        twin,
        at(z + 1 - 2 * (z % 2), xh, y, a, c),
        at(3 - z, xh, y, a, c),
        other_h,
    )

    def offset_start():
        obs[0] = jnp.broadcast_to(jnp.sum(oacc[...].reshape(128, 128).T, axis=0, keepdims=True), (8, 128))
        send("o", 0, obs.at[0], obr.at[0], partners[0])

    def offset_step(k):
        if k == 0:
            offset_start()
            return
        arrive("o", k - 1)
        if k < 4:
            obs[k] = obs[k - 1] + obr[k - 1]
            send("o", k, obs.at[k], obr.at[k], partners[k])
        else:
            total = obs[k - 1] + obr[k - 1]
            off[...] = jnp.where(c == 0, total[0:1, 0:64], total[0:1, 64:128])

    table = dict(
        lam=step_lam, downx=step_downx, downy=step_downy, x1=step_x1, y1=step_y1, x2=step_x2, y2=step_y2,
        x3=step_x3, y3=step_y3, gx1=step_gx1, gy1=step_gy1, gx2=step_gx2, gy2=step_gy2, gx3=step_gx3, gy3=step_gy3,
        mma=step_mma, mm=step_mm, z1=step_z1, out=step_out, w=weights, o=offset_step,
    )
    for name, r in PLAN:
        table[name](r)
    for copy in copies.values():
        copy.wait_send()


def per_device(
    spec_rows, readout, gate_weight, up_weight, down_weight, gate_lo, gate_width, up_lo, up_width, flags
):
    d_own = readout.shape[1]
    units = down_weight.shape[0]
    half = units // 2
    cx = 768
    cy = half - cx
    rows = 8 * OWN
    r = CHUNKS
    lanes = [value.reshape(units // 128, 128) for value in (gate_lo, gate_width, up_lo, up_width, flags)]
    vm = pltpu.VMEM
    scratch = [
        vm((readout.shape[0], d_own), BF16),
        vm((d_own, units), BF16),
        vm((d_own, units), BF16),
        vm((half, 2 * d_own), BF16),
        vm((spec_rows.shape[0], 8), F32),
        vm((rows, readout.shape[0]), BF16),
        vm((r, rows, 2 * d_own), BF16),
        vm((5, 32, 128), F32),
        vm((r, 8, OWN, cx), F32),
        vm((r, 2, 4, OWN, cy), F32),
        vm((r, 4, OWN, cx), BF16),
        vm((r, 4, OWN, cx), BF16),
        vm((r, 2, OWN, cx), BF16),
        vm((r, 2, OWN, cx), BF16),
        vm((r, 2, HALF, cx), BF16),
        vm((r, 2, HALF, cx), BF16),
        vm((r, 2, 2, OWN, cy), BF16),
        vm((r, 2, 2, OWN, cy), BF16),
        vm((r, 2, 2, HALF, cy), BF16),
        vm((r, 2, 2, HALF, cy), BF16),
        vm((r, OWN, cy), BF16),
        vm((r, OWN, cy), BF16),
        vm((r, 2, 2, 4, OWN, cx), BF16),
        vm((r, 2, 2, 4, OWN, cy), BF16),
        vm((r, 2, 4, OWN, d_own), F32),
        vm((r, 3, 2, OWN, d_own), F32),
        vm((r, OWN, d_own), F32),
        vm((r, OWN, d_own), F32),
        vm((2, 4, OWN, d_own), BF16),
        vm((8, OWN, d_own), BF16),
        vm((2, r, HALF, 128), F32),
        vm((4, 8, 128), F32),
        vm((4, 8, 128), F32),
        pltpu.SemaphoreType.DMA((5,)),
        pltpu.SemaphoreType.DMA((48, r)),
        pltpu.SemaphoreType.DMA((48, r)),
    ]
    held = pl.BlockSpec(memory_space=pltpu.VMEM)
    far = pl.BlockSpec(memory_space=pl.ANY)
    coeffs, offsets = pl.pallas_call(
        kernel,
        name="bound_pass",
        out_shape=(
            jax.ShapeDtypeStruct((spec_rows.shape[0] // 8, d_own), F32),
            jax.ShapeDtypeStruct((1, 64), F32),
        ),
        in_specs=[held, far, far, far, far, held, held, held, held, held],
        out_specs=(held, held),
        scratch_shapes=scratch,
        compiler_params=pltpu.CompilerParams(
            collective_id=0, has_side_effects=True, vmem_limit_bytes=60 * 1024 * 1024
        ),
    )(spec_rows.T, readout, gate_weight, up_weight, down_weight, *lanes)
    return coeffs, offsets.reshape(64)


def solution(mesh):
    placed = (
        P(),
        P(None, "wid"),
        P("wid", "hid"),
        P("wid", "hid"),
        P("hid", "wid"),
        P("hid"),
        P("hid"),
        P("hid"),
        P("hid"),
        P("hid"),
    )
    return jax.shard_map(
        per_device,
        mesh=mesh,
        in_specs=placed,
        out_specs=(P("hid", "wid"), P("wid")),
        check_vma=False,
    )
```

```python
import jax
import jax.numpy as jnp
from jax import lax
from jax.experimental import pallas as pl
from jax.experimental.pallas import tpu as pltpu
from jax.sharding import PartitionSpec as P

MESH = pl.DeviceIdType.MESH
F32 = jnp.float32
BF16 = jnp.bfloat16
NT = (((1,), (1,)), ((), ()))

CHUNKS = 4
OWN = 32
HALF = OWN // 2


def silu(value):
    return value / (1.0 + jnp.exp(-value))


def unit_tables(gate_lo, gate_width, up_lo, up_width, flags):
    gate_hi = gate_lo + gate_width
    up_hi = up_lo + up_width
    middle = 0.5 * (gate_lo + gate_hi)
    valley = jnp.clip(-1.2784645, gate_lo, gate_hi)
    silu_lo = silu(gate_lo)
    silu_hi = silu(gate_hi)
    silu_valley = silu(valley)
    s_low = jnp.minimum(jnp.minimum(silu_lo, silu_hi), silu_valley)
    s_high = jnp.maximum(silu_lo, silu_hi)
    slope = (silu_hi - silu_lo) / gate_width
    rest_a = silu_lo - slope * gate_lo
    rest_b = silu(middle) - slope * middle
    rest_c = silu_valley - slope * valley
    b_low = jnp.minimum(jnp.minimum(rest_a, rest_b), rest_c)
    b_high = jnp.maximum(jnp.maximum(rest_a, rest_b), rest_c)
    second = flags == 1
    as_lower = jnp.where(second, up_hi, up_lo)
    as_upper = jnp.where(second, up_lo, up_hi)
    au = jnp.where(second, s_high, s_low)
    kp = jnp.maximum(as_lower, 0.0) * b_low + jnp.minimum(as_lower, 0.0) * b_high - au * as_lower
    kn = jnp.minimum(as_upper, 0.0) * b_low + jnp.maximum(as_upper, 0.0) * b_high - au * as_upper
    return au, as_lower * slope, as_upper * slope, kp, kn


PLAN = (
    ("lam", 0), ("lam", 1), ("downx", 0), ("downy", 0), ("lam", 2), ("downx", 1), ("downy", 1), ("y1", 0),
    ("lam", 3), ("x1", 0), ("downx", 2), ("y1", 1), ("y2", 0), ("x1", 1), ("x2", 0), ("downy", 2), ("y2", 1),
    ("downx", 3), ("x2", 1), ("x3", 0), ("y3", 0), ("x1", 2), ("y3", 1), ("y1", 2), ("x3", 1), ("downy", 3),
    ("gy1", 0), ("gx1", 0), ("gy1", 1), ("w", 0), ("gx2", 0), ("x2", 2), ("y2", 2), ("x1", 3), ("gy2", 0),
    ("gx1", 1), ("y1", 3), ("gx3", 0), ("y3", 2), ("w", 1), ("x3", 2), ("gx2", 1), ("x2", 3), ("gy3", 0),
    ("mma", 0), ("gy2", 1), ("y2", 3), ("gy1", 2), ("mm", 0), ("x3", 3), ("gx1", 2), ("gy3", 1), ("y3", 3),
    ("o", 0), ("gx3", 1), ("gy2", 2), ("mma", 1), ("gx2", 2), ("mm", 1), ("gx1", 3), ("o", 1), ("gy1", 3),
    ("gx3", 2), ("gy3", 2), ("z1", 0), ("mma", 2), ("mm", 2), ("gx3", 3), ("gy3", 3), ("o", 2), ("mma", 3),
    ("z1", 1), ("mm", 3), ("o", 3), ("out", 0), ("out", 2), ("out", 1), ("o", 4), ("out", 3),
)
STRAIGHT = (2, 3)
SPREAD = (3,)


def kernel(
    spec, readout, gate, up, down, gate_lo, gate_width, up_lo, up_width, flags,
    out, off,
    ro, wp, wn, dn, pairs, oh, lam, tab,
    px, py, x1s, x1r, xps, xpr, xqs, xqr, yps, ypr, yqs, yqr, yxs, yxr,
    lx, ly, acc, zr, hs, hr, ends, endr, oacc, obs, obr,
    lsem, ssem, rsem,
):
    hid, wid = lax.axis_index("hid"), lax.axis_index("wid")
    z, xh = hid // 2, hid % 2
    y, a, c = wid // 4, (wid // 2) % 2, wid % 2
    half = dn.shape[0]
    cx, cy = px.shape[-1], py.shape[-1]
    d_own = ro.shape[1]
    rows = 8 * OWN
    mine, its = pl.ds(0, d_own), pl.ds(d_own, d_own)
    yu, yd, yo = (y + 1) % 4, (y + 3) % 4, (y + 2) % 4
    zu, zd, zo = (z + 1) % 4, (z + 3) % 4, (z + 2) % 4

    def at(z_, xh_, y_, a_, c_):
        return (z_ * 2 + xh_, (y_ * 2 + a_) * 2 + c_)

    up_y, down_y = at(z, xh, yu, a, c), at(z, xh, yd, a, c)
    other_x = at(z, xh, y, 1 - a, c)
    twin = at(z, xh, y, a, 1 - c)
    over_y = at(z, xh, yo, a, c)
    by_z = {(s, f): at((z + s) % 4, (xh + f) % 2, y, a, c) for s in range(4) for f in range(2) if s or f}
    other_h = by_z[0, 1]

    barrier = pltpu.get_barrier_semaphore()
    for device in (up_y, down_y, over_y, other_x, twin, *by_z.values()):
        pl.semaphore_signal(barrier, inc=1, device_id=device, device_id_type=MESH)

    load_ro = pltpu.make_async_copy(readout, ro, lsem.at[0])
    load_ro.start()
    my_half = pl.multiple_of(c * half, half)
    its_half = pl.multiple_of((1 - c) * half, half)
    load_dx = pltpu.make_async_copy(down.at[pl.ds(my_half, cx)], dn.at[pl.ds(0, cx), mine], lsem.at[1])
    load_dy = pltpu.make_async_copy(
        down.at[pl.ds(pl.multiple_of(my_half + cx, 256), cy)], dn.at[pl.ds(cx, cy), mine], lsem.at[2]
    )
    load_dx.start()
    load_dy.start()
    load_up = pltpu.make_async_copy(up, wp, lsem.at[3])
    load_gate = pltpu.make_async_copy(gate, wn, lsem.at[4])

    copies = {}
    unsent = {}
    index = {}

    def send(name, r, src, dst, device):
        if (name, r - 2) in unsent:
            unsent.pop((name, r - 2)).wait_send()
        k = index.setdefault((name, r % 2), len(index))
        copy = pltpu.make_async_remote_copy(
            src_ref=src, dst_ref=dst, send_sem=ssem.at[k], recv_sem=rsem.at[len(copies)],
            device_id=device, device_id_type=MESH,
        )
        copy.start()
        copies[name, r] = unsent[name, r] = copy

    def arrive(name, r):
        copies[name, r].wait_recv()

    for k, table in enumerate(
        unit_tables(gate_lo[...], gate_width[...], up_lo[...], up_width[...], flags[...])
    ):
        tab[k, 0 : table.shape[0], :] = table

    tall = jnp.concatenate([spec[...].astype(F32), jnp.zeros((6, spec.shape[1]), F32)], axis=0)
    pairs[...] = tall.T
    oacc[...] = jnp.zeros_like(oacc)

    def pick_rows(r):
        def group(g, carry):
            a_, y_, co = g // 8, (g // 2) % 4, g % 2
            start = pl.multiple_of((y_ * 2 + a_) * 128 + co * 64 + r * 16, 16)
            pair = pairs[pl.ds(start, 16), :].astype(jnp.int32)
            classes = lax.broadcasted_iota(jnp.int32, (16, ro.shape[0]), 1)
            picked = jnp.where(classes == pair[:, 0:1], 1.0, 0.0) - jnp.where(classes == pair[:, 1:2], 1.0, 0.0)
            oh[pl.ds(pl.multiple_of(g * 16, 16), 16), :] = picked.astype(BF16)
            return carry

        lax.fori_loop(0, 16, group, 0)

    def lam_rows(r):
        lam[r, :, 0:d_own] = jnp.dot(oh[...], ro[...], preferred_element_type=F32).astype(BF16)

    def tree_first(stage, get, u, d, o):
        lead = (slice(None),) * (len(stage.shape) - 3)
        stage[(0, *lead, slice(0, HALF))] = get(o, 0).astype(stage.dtype)
        stage[(0, *lead, slice(HALF, OWN))] = get(u, 1).astype(stage.dtype)
        stage[(1, *lead, slice(0, HALF))] = get(d, 0).astype(stage.dtype)
        stage[(1, *lead, slice(HALF, OWN))] = get(o, 1).astype(stage.dtype)

    def tree_second(stage, came, get, u, d):
        lead = (slice(None),) * (len(came.shape) - 3)
        stage[0] = (get(u, 0) + came[(0, *lead, slice(0, HALF))].astype(F32)).astype(stage.dtype)
        stage[1] = (get(d, 1) + came[(1, *lead, slice(HALF, OWN))].astype(F32)).astype(stage.dtype)

    def tree_last(came, second, get, own):
        lead = (slice(None),) * (len(came.shape) - 3)
        low = get(own, 0) + came[(1, *lead, slice(0, HALF))].astype(F32) + second[0].astype(F32)
        high = get(own, 1) + came[(0, *lead, slice(HALF, OWN))].astype(F32) + second[1].astype(F32)
        return low, high

    def halves(h):
        return slice(h * HALF, (h + 1) * HALF)

    def get_x(r):
        return lambda y_, h: px[r, a * 4 + y_, halves(h)]

    def get_y(r):
        return lambda y_, h: py[r, :, y_, halves(h)]

    def get_z(r):
        return lambda z_, h: acc[r, :, z_, halves(h)]

    def constant_terms(r, h, value, first):
        blocks = value.shape[-1] // 128
        total = jnp.zeros((HALF, 128), F32)
        for j in range(blocks):
            row = c * (half // 128) + first + j
            part = value[:, j * 128 : (j + 1) * 128]
            total = total + jnp.maximum(part, 0.0) * tab[3, pl.ds(row, 1), :]
            total = total + jnp.minimum(part, 0.0) * tab[4, pl.ds(row, 1), :]
        oacc[h, r] += total

    def step_lam(r):
        pick_rows(r)
        if r == 0:
            pl.semaphore_wait(barrier, 5 + len(by_z))
            send("dx", 0, down.at[pl.ds(its_half, cx)], dn.at[pl.ds(0, cx), its], twin)
            later = pl.ds(pl.multiple_of(its_half + cx, 256), cy)
            send("dy", 0, down.at[later], dn.at[pl.ds(cx, cy), its], twin)
            load_ro.wait()
        lam_rows(r)
        send("lam", r, lam.at[r, :, mine], lam.at[r, :, its], twin)

    def times_down(r, units):
        return lax.dot_general(lam[r], dn[units, :], NT, preferred_element_type=F32)

    def step_downx(r):
        if r == 0:
            load_dx.wait()
            arrive("dx", 0)
        arrive("lam", r)
        for n in range(cx // 256):
            columns = slice(n * 256, (n + 1) * 256)
            px[r, :, :, columns] = times_down(r, columns).reshape(8, OWN, 256)
        x1s[r] = px[r, pl.ds((1 - a) * 4, 4)].astype(BF16)
        send("x1", r, x1s.at[r], x1r.at[r], other_x)

    def step_downy(r):
        if r == 0:
            load_up.start()
            load_gate.start()
            load_dy.wait()
            arrive("dy", 0)
        for n in range(cy // 256):
            columns = slice(n * 256, (n + 1) * 256)
            units = slice(cx + n * 256, cx + (n + 1) * 256)
            py[r, :, :, :, columns] = times_down(r, units).reshape(2, 4, OWN, 256)
        tree_first(yps.at[r], get_y(r), yu, yd, yo)
        send("yu1", r, yps.at[r, 0], ypr.at[r, 0], up_y)
        send("yd1", r, yps.at[r, 1], ypr.at[r, 1], down_y)

    def step_x1(r):
        arrive("x1", r)
        own = pl.ds(a * 4, 4)
        px[r, own] += x1r[r].astype(F32)
        tree_first(xps.at[r], get_x(r), yu, yd, yo)
        send("xu1", r, xps.at[r, 0], xpr.at[r, 0], up_y)
        send("xd1", r, xps.at[r, 1], xpr.at[r, 1], down_y)

    def step_y1(r):
        arrive("yu1", r)
        arrive("yd1", r)
        tree_second(yqs.at[r], ypr.at[r], get_y(r), yu, yd)
        send("yu2", r, yqs.at[r, 0], yqr.at[r, 0], up_y)
        send("yd2", r, yqs.at[r, 1], yqr.at[r, 1], down_y)

    def step_x2(r):
        arrive("xu1", r)
        arrive("xd1", r)
        tree_second(xqs.at[r], xpr.at[r], get_x(r), yu, yd)
        send("xu2", r, xqs.at[r, 0], xqr.at[r, 0], up_y)
        send("xd2", r, xqs.at[r, 1], xqr.at[r, 1], down_y)

    def step_y2(r):
        arrive("yu2", r)
        arrive("yd2", r)
        low, high = tree_last(ypr.at[r], yqr.at[r], get_y(r), y)
        py[r, :, y, halves(0)] = low
        py[r, :, y, halves(1)] = high
        yxs[r] = py[r, 1 - a, y].astype(BF16)
        send("yx", r, yxs.at[r], yxr.at[r], other_x)

    def step_x3(r):
        arrive("xu2", r)
        arrive("xd2", r)
        for h, value in enumerate(tree_last(xpr.at[r], xqr.at[r], get_x(r), y)):
            lx[r, c, a, y, halves(h)] = value.astype(BF16)
            constant_terms(r, h, value, 0)
        block = lx.at[r, c, a, y]
        send("gxu1", r, block, block, up_y)
        send("gxd1", r, block, block, down_y)
        send("gxx0", r, block, block, other_x)
        if r in SPREAD:
            send("gxo", r, block, block, over_y)

    def step_y3(r):
        arrive("yx", r)
        for h in range(2):
            value = py[r, a, y, halves(h)] + yxr[r, halves(h)].astype(F32)
            ly[r, c, a, y, halves(h)] = value.astype(BF16)
            constant_terms(r, h, value, cx // 128)
        block = ly.at[r, c, a, y]
        send("gyx", r, block, block, other_x)
        send("gyu1", r, block, block, up_y)
        send("gyd1", r, block, block, down_y)
        if r in SPREAD:
            send("gyo", r, block, block, over_y)

    def step_gx1(r):
        arrive("gxu1", r)
        arrive("gxd1", r)
        if r in SPREAD:
            arrive("gxo", r)
            for name, y_ in (("gxx1", yu), ("gxx2", yd), ("gxx3", yo)):
                block = lx.at[r, c, a, y_]
                send(name, r, block, block, other_x)
            block = lx.at[r, c, a]
            send("tx0", r, block, block, twin)
            return
        below = lx.at[r, c, a, yd, halves(0)]
        above = lx.at[r, c, a, yu, halves(1)]
        send("gxu2", r, below, below, up_y)
        send("gxd2", r, above, above, down_y)
        for name, y_ in (("gxx1", yu), ("gxx2", yd)):
            block = lx.at[r, c, a, y_]
            send(name, r, block, block, other_x)

    def step_gy1(r):
        arrive("gyx", r)
        block = ly.at[r, c, 1 - a, y]
        send("gyu1b", r, block, block, up_y)
        send("gyd1b", r, block, block, down_y)
        if r in SPREAD:
            send("gyob", r, block, block, over_y)

    def step_gx2(r):
        arrive("gxu2", r)
        arrive("gxd2", r)
        block = lx.at[r, c, a, yo]
        send("gxx3", r, block, block, other_x)
        block = lx.at[r, c, a]
        send("tx0", r, block, block, twin)

    def step_gy2(r):
        for name in ("gyu1", "gyd1", "gyu1b", "gyd1b"):
            arrive(name, r)
        below = ly.at[r, c, :, yd, halves(0)]
        above = ly.at[r, c, :, yu, halves(1)]
        send("gyu2", r, below, below, up_y)
        send("gyd2", r, above, above, down_y)

    def step_gx3(r):
        for k in range(4):
            arrive("gxx%d" % k, r)
        block = lx.at[r, c, 1 - a]
        send("tx1", r, block, block, twin)

    def step_gy3(r):
        if r in SPREAD:
            for name in ("gyu1", "gyd1", "gyu1b", "gyd1b", "gyo", "gyob"):
                arrive(name, r)
        else:
            arrive("gyu2", r)
            arrive("gyd2", r)
        block = ly.at[r, c]
        send("ty", r, block, block, twin)

    def times_weights(r, cc, add):
        base = cc * half
        columns_x = pl.ds(pl.multiple_of(base, 256), cx)
        columns_y = pl.ds(pl.multiple_of(base + cx, 256), cy)

        def block(n, carry):
            units = pl.ds(pl.multiple_of(n * 256, 256), 256)
            total = None
            for ref, columns in ((lx, columns_x), (ly, columns_y)):
                value = ref[r, cc].reshape(rows, columns.size)
                for part, weight in ((jnp.maximum(value, 0), wp), (jnp.minimum(value, 0), wn)):
                    term = lax.dot_general(part, weight[units, columns], NT, preferred_element_type=F32)
                    total = term if total is None else total + term
            total = total.reshape(2, 4, OWN, 256)
            if add:
                acc[r, :, :, :, units] += total
            else:
                acc[r, :, :, :, units] = total
            return carry

        lax.fori_loop(0, d_own // 256, block, 0, unroll=True)

    def step_mma(r):
        times_weights(r, c, False)

    def step_mm(r):
        arrive("tx0", r)
        arrive("tx1", r)
        arrive("ty", r)
        times_weights(r, 1 - c, True)
        if r in STRAIGHT:
            k = STRAIGHT.index(r)
            ends[k] = acc[r].astype(BF16)
            for (s, f), device in by_z.items():
                send("e%d%d" % (s, f), r, ends.at[k, (xh + f) % 2, (z + s) % 4], endr.at[k, s * 2 + f], device)
        else:
            for s, z_ in ((1, zu), (3, zd), (2, zo)):
                send("z%d" % s, r, acc.at[r, :, z_], zr.at[r, s - 1], by_z[s, 0])

    def step_z1(r):
        for s in (1, 3, 2):
            arrive("z%d" % s, r)
        hs[r] = (acc[r, 1 - xh, z] + zr[r, 0, 1 - xh]) + (zr[r, 1, 1 - xh] + zr[r, 2, 1 - xh])
        send("h", r, hs.at[r], hr.at[r], other_h)

    def drain(keys):
        for key in keys:
            unsent.pop(key).wait_send()

    def step_out(r):
        if r == CHUNKS - 1:
            drain(tuple(key for key in unsent if key[0][0] not in "hez"))
        first = pl.multiple_of((xh * 4 + z) * OWN, OWN)
        total = lam[r, pl.ds(first, OWN), 0:d_own].astype(F32) + acc[r, xh, z]
        if r in STRAIGHT:
            for s, f in by_z:
                arrive("e%d%d" % (s, f), r)
                total = total + endr[STRAIGHT.index(r), s * 2 + f].astype(F32)
        else:
            total = total + (zr[r, 0, xh] + zr[r, 1, xh] + zr[r, 2, xh])
            arrive("h", r)
            total = total + hr[r]
        for h in range(2):
            out[h * 64 + r * HALF : h * 64 + (r + 1) * HALF, :] = total[halves(h)]

    def weights(k):
        if k == 0:
            load_up.wait()
            load_gate.wait()

        def block(j, carry):
            columns = pl.ds(pl.multiple_of(j * 128, 128), 128)
            scaled = wp[:, columns].astype(F32) * tab[0, pl.ds(j, 1), :]
            gates = wn[:, columns].astype(F32)
            wp[:, columns] = (scaled + gates * tab[1, pl.ds(j, 1), :]).astype(BF16)
            wn[:, columns] = (scaled + gates * tab[2, pl.ds(j, 1), :]).astype(BF16)
            return carry

        count = wp.shape[1] // 128 // 2
        lax.fori_loop(k * count, (k + 1) * count, block, 0)

    partners = (
        twin,
        at(z + 1 - 2 * (z % 2), xh, y, a, c),
        at(3 - z, xh, y, a, c),
        other_h,
    )

    def offset_start():
        obs[0] = jnp.broadcast_to(jnp.sum(oacc[...].reshape(128, 128).T, axis=0, keepdims=True), (8, 128))
        send("o", 0, obs.at[0], obr.at[0], partners[0])

    def offset_step(k):
        if k == 0:
            offset_start()
            return
        arrive("o", k - 1)
        if k < 4:
            obs[k] = obs[k - 1] + obr[k - 1]
            send("o", k, obs.at[k], obr.at[k], partners[k])
        else:
            total = obs[k - 1] + obr[k - 1]
            off[...] = jnp.where(c == 0, total[0:1, 0:64], total[0:1, 64:128])

    table = dict(
        lam=step_lam, downx=step_downx, downy=step_downy, x1=step_x1, y1=step_y1, x2=step_x2, y2=step_y2,
        x3=step_x3, y3=step_y3, gx1=step_gx1, gy1=step_gy1, gx2=step_gx2, gy2=step_gy2, gx3=step_gx3, gy3=step_gy3,
        mma=step_mma, mm=step_mm, z1=step_z1, out=step_out, w=weights, o=offset_step,
    )
    for name, r in PLAN:
        table[name](r)
    drain(tuple(unsent))


def hand_over(coeffs, offsets, out, off):
    out[...] = coeffs[...]
    off[...] = offsets[...]


def per_device(
    spec_rows, readout, gate_weight, up_weight, down_weight, gate_lo, gate_width, up_lo, up_width, flags
):
    d_own = readout.shape[1]
    units = down_weight.shape[0]
    half = units // 2
    cx = 768
    cy = half - cx
    rows = 8 * OWN
    r = CHUNKS
    lanes = [value.reshape(units // 128, 128) for value in (gate_lo, gate_width, up_lo, up_width, flags)]
    vm = pltpu.VMEM
    scratch = [
        vm((readout.shape[0], d_own), BF16),
        vm((d_own, units), BF16),
        vm((d_own, units), BF16),
        vm((half, 2 * d_own), BF16),
        vm((spec_rows.shape[0], 8), F32),
        vm((rows, readout.shape[0]), BF16),
        vm((r, rows, 2 * d_own), BF16),
        vm((5, 32, 128), F32),
        vm((r, 8, OWN, cx), F32),
        vm((r, 2, 4, OWN, cy), F32),
        vm((r, 4, OWN, cx), BF16),
        vm((r, 4, OWN, cx), BF16),
        vm((r, 2, OWN, cx), BF16),
        vm((r, 2, OWN, cx), BF16),
        vm((r, 2, HALF, cx), BF16),
        vm((r, 2, HALF, cx), BF16),
        vm((r, 2, 2, OWN, cy), BF16),
        vm((r, 2, 2, OWN, cy), BF16),
        vm((r, 2, 2, HALF, cy), BF16),
        vm((r, 2, 2, HALF, cy), BF16),
        vm((r, OWN, cy), BF16),
        vm((r, OWN, cy), BF16),
        vm((r, 2, 2, 4, OWN, cx), BF16),
        vm((r, 2, 2, 4, OWN, cy), BF16),
        vm((r, 2, 4, OWN, d_own), F32),
        vm((r, 3, 2, OWN, d_own), F32),
        vm((r, OWN, d_own), F32),
        vm((r, OWN, d_own), F32),
        vm((len(STRAIGHT), 2, 4, OWN, d_own), BF16),
        vm((len(STRAIGHT), 8, OWN, d_own), BF16),
        vm((2, r, HALF, 128), F32),
        vm((4, 8, 128), F32),
        vm((4, 8, 128), F32),
        pltpu.SemaphoreType.DMA((5,)),
        pltpu.SemaphoreType.DMA((96,)),
        pltpu.SemaphoreType.DMA((160,)),
    ]
    held = pl.BlockSpec(memory_space=pltpu.VMEM)
    far = pl.BlockSpec(memory_space=pl.ANY)
    coeffs, offsets = pl.pallas_call(
        kernel,
        name="bound_pass",
        out_shape=(
            jax.ShapeDtypeStruct((spec_rows.shape[0] // 8, d_own), F32),
            jax.ShapeDtypeStruct((1, 64), F32),
        ),
        in_specs=[held, far, far, far, far, held, held, held, held, held],
        out_specs=(held, held),
        scratch_shapes=scratch,
        compiler_params=pltpu.CompilerParams(
            collective_id=0, has_side_effects=True, vmem_limit_bytes=60 * 1024 * 1024
        ),
    )(spec_rows.T, readout, gate_weight, up_weight, down_weight, *lanes)
    coeffs, offsets = pl.pallas_call(
        hand_over,
        name="hand_over",
        out_shape=(jax.ShapeDtypeStruct(coeffs.shape, F32), jax.ShapeDtypeStruct(offsets.shape, F32)),
        in_specs=[held, held],
        out_specs=(held, held),
    )(coeffs, offsets)
    return coeffs, offsets.reshape(64)


def solution(mesh):
    placed = (
        P(),
        P(None, "wid"),
        P("wid", "hid"),
        P("wid", "hid"),
        P("hid", "wid"),
        P("hid"),
        P("hid"),
        P("hid"),
        P("hid"),
        P("hid"),
    )
    return jax.shard_map(
        per_device,
        mesh=mesh,
        in_specs=placed,
        out_specs=(P("hid", "wid"), P("wid")),
        check_vma=False,
    )
```

```python
import jax
import jax.numpy as jnp
from jax import lax
from jax.experimental import pallas as pl
from jax.experimental.pallas import tpu as pltpu
from jax.sharding import PartitionSpec as P

MESH = pl.DeviceIdType.MESH
F32 = jnp.float32
BF16 = jnp.bfloat16
NT = (((1,), (1,)), ((), ()))

CHUNKS = 4
OWN = 32
HALF = OWN // 2


def silu(value):
    return value / (1.0 + jnp.exp(-value))


def unit_tables(gate_lo, gate_width, up_lo, up_width, flags):
    gate_hi = gate_lo + gate_width
    up_hi = up_lo + up_width
    middle = 0.5 * (gate_lo + gate_hi)
    valley = jnp.clip(-1.2784645, gate_lo, gate_hi)
    silu_lo = silu(gate_lo)
    silu_hi = silu(gate_hi)
    silu_valley = silu(valley)
    s_low = jnp.minimum(jnp.minimum(silu_lo, silu_hi), silu_valley)
    s_high = jnp.maximum(silu_lo, silu_hi)
    slope = (silu_hi - silu_lo) / gate_width
    rest_a = silu_lo - slope * gate_lo
    rest_b = silu(middle) - slope * middle
    rest_c = silu_valley - slope * valley
    b_low = jnp.minimum(jnp.minimum(rest_a, rest_b), rest_c)
    b_high = jnp.maximum(jnp.maximum(rest_a, rest_b), rest_c)
    second = flags == 1
    as_lower = jnp.where(second, up_hi, up_lo)
    as_upper = jnp.where(second, up_lo, up_hi)
    au = jnp.where(second, s_high, s_low)
    kp = jnp.maximum(as_lower, 0.0) * b_low + jnp.minimum(as_lower, 0.0) * b_high - au * as_lower
    kn = jnp.minimum(as_upper, 0.0) * b_low + jnp.maximum(as_upper, 0.0) * b_high - au * as_upper
    return au, as_lower * slope, as_upper * slope, kp, kn


PLAN = (
    ("lam", 0), ("lam", 1), ("downx", 0), ("downy", 0), ("lam", 2), ("downx", 1), ("downy", 1), ("lam", 3),
    ("y1", 0), ("downx", 2), ("x1", 0), ("downy", 2), ("y1", 1), ("downx", 3), ("y2", 0), ("x2", 0), ("downy", 3),
    ("x1", 1), ("x3", 0), ("x2", 1), ("x1", 2), ("y2", 1), ("y1", 2), ("y3", 0), ("w", 0), ("gx1", 0), ("x3", 1),
    ("x1", 3), ("y1", 3), ("x2", 2), ("y3", 1), ("gx2", 0), ("y2", 2), ("gy1", 0), ("gx1", 1), ("gy1", 1),
    ("gx3", 0), ("x3", 2), ("y2", 3), ("gy2", 0), ("w", 1), ("x2", 3), ("gx2", 1), ("y3", 2), ("gy2", 1),
    ("gy3", 0), ("x3", 3), ("y3", 3), ("o", 0), ("mma", 0), ("mm", 0), ("gy1", 2), ("gx1", 2), ("gx3", 1),
    ("gy3", 1), ("mma", 1), ("gx1", 3), ("o", 1), ("gy1", 3), ("gx2", 2), ("gy2", 2), ("mm", 1), ("gx2", 3),
    ("gy2", 3), ("gx3", 2), ("gy3", 2), ("z1", 0), ("mma", 2), ("gx3", 3), ("gy3", 3), ("o", 2), ("mm", 2),
    ("mma", 3), ("mm", 3), ("o", 3), ("z1", 1), ("out", 0), ("out", 1), ("out", 2), ("o", 4), ("out", 3),
)
STRAIGHT = (2, 3)
SPREAD = ()


def kernel(
    spec, readout, gate, up, down, gate_lo, gate_width, up_lo, up_width, flags,
    out, off,
    ro, wp, wn, dn, dt, pairs, oh, lam, tab,
    px, py, x1s, x1r, xps, xpr, xqs, xqr, yps, ypr, yqs, yqr, yxs, yxr,
    lx, ly, acc, zr, hs, hr, ends, endr, oacc, obs, obr,
    lsem, ssem, rsem,
):
    hid, wid = lax.axis_index("hid"), lax.axis_index("wid")
    z, xh = hid // 2, hid % 2
    y, a, c = wid // 4, (wid // 2) % 2, wid % 2
    half = dn.shape[0]
    cx, cy = px.shape[-1], py.shape[-1]
    d_own = ro.shape[1]
    rows = 8 * OWN
    mine, its = pl.ds(0, d_own), pl.ds(d_own, d_own)
    yu, yd, yo = (y + 1) % 4, (y + 3) % 4, (y + 2) % 4
    zu, zd, zo = (z + 1) % 4, (z + 3) % 4, (z + 2) % 4

    def at(z_, xh_, y_, a_, c_):
        return (z_ * 2 + xh_, (y_ * 2 + a_) * 2 + c_)

    up_y, down_y = at(z, xh, yu, a, c), at(z, xh, yd, a, c)
    other_x = at(z, xh, y, 1 - a, c)
    twin = at(z, xh, y, a, 1 - c)
    over_y = at(z, xh, yo, a, c)
    by_z = {(s, f): at((z + s) % 4, (xh + f) % 2, y, a, c) for s in range(4) for f in range(2) if s or f}
    other_h = by_z[0, 1]

    barrier = pltpu.get_barrier_semaphore()
    for device in (up_y, down_y, over_y, other_x, twin, *by_z.values()):
        pl.semaphore_signal(barrier, inc=1, device_id=device, device_id_type=MESH)

    load_ro = pltpu.make_async_copy(readout, ro, lsem.at[0])
    load_ro.start()
    my_half = pl.multiple_of(c * half, half)
    its_half = pl.multiple_of((1 - c) * half, half)
    load_dx = pltpu.make_async_copy(down.at[pl.ds(my_half, cx)], dn.at[pl.ds(0, cx), mine], lsem.at[1])
    load_dy = pltpu.make_async_copy(
        down.at[pl.ds(pl.multiple_of(my_half + cx, 256), cy)], dn.at[pl.ds(cx, cy), mine], lsem.at[2]
    )
    load_tx = pltpu.make_async_copy(down.at[pl.ds(its_half, cx)], dt.at[pl.ds(0, cx)], lsem.at[5])
    load_ty = pltpu.make_async_copy(
        down.at[pl.ds(pl.multiple_of(its_half + cx, 256), cy)], dt.at[pl.ds(cx, cy)], lsem.at[6]
    )
    load_tx.start()
    load_dx.start()
    load_ty.start()
    load_dy.start()
    load_up = pltpu.make_async_copy(up, wp, lsem.at[3])
    load_gate = pltpu.make_async_copy(gate, wn, lsem.at[4])

    copies = {}
    unsent = {}
    index = {}

    def send(name, r, src, dst, device):
        if (name, r - 2) in unsent:
            unsent.pop((name, r - 2)).wait_send()
        k = index.setdefault((name, r % 2), len(index))
        copy = pltpu.make_async_remote_copy(
            src_ref=src, dst_ref=dst, send_sem=ssem.at[k], recv_sem=rsem.at[len(copies)],
            device_id=device, device_id_type=MESH,
        )
        copy.start()
        copies[name, r] = unsent[name, r] = copy

    def arrive(name, r):
        copies[name, r].wait_recv()

    for k, table in enumerate(
        unit_tables(gate_lo[...], gate_width[...], up_lo[...], up_width[...], flags[...])
    ):
        tab[k, 0 : table.shape[0], :] = table

    tall = jnp.concatenate([spec[...].astype(F32), jnp.zeros((6, spec.shape[1]), F32)], axis=0)
    pairs[...] = tall.T
    oacc[...] = jnp.zeros_like(oacc)

    def pick_rows(r):
        def group(g, carry):
            a_, y_, co = g // 8, (g // 2) % 4, g % 2
            start = pl.multiple_of((y_ * 2 + a_) * 128 + co * 64 + r * 16, 16)
            pair = pairs[pl.ds(start, 16), :].astype(jnp.int32)
            classes = lax.broadcasted_iota(jnp.int32, (16, ro.shape[0]), 1)
            picked = jnp.where(classes == pair[:, 0:1], 1.0, 0.0) - jnp.where(classes == pair[:, 1:2], 1.0, 0.0)
            oh[pl.ds(pl.multiple_of(g * 16, 16), 16), :] = picked.astype(BF16)
            return carry

        lax.fori_loop(0, 16, group, 0)

    def lam_rows(r):
        lam[r, :, 0:d_own] = jnp.dot(oh[...], ro[...], preferred_element_type=F32).astype(BF16)

    def tree_first(stage, get, u, d, o):
        lead = (slice(None),) * (len(stage.shape) - 3)
        stage[(0, *lead, slice(0, HALF))] = get(o, 0).astype(stage.dtype)
        stage[(0, *lead, slice(HALF, OWN))] = get(u, 1).astype(stage.dtype)
        stage[(1, *lead, slice(0, HALF))] = get(d, 0).astype(stage.dtype)
        stage[(1, *lead, slice(HALF, OWN))] = get(o, 1).astype(stage.dtype)

    def tree_second(stage, came, get, u, d):
        lead = (slice(None),) * (len(came.shape) - 3)
        stage[0] = (get(u, 0) + came[(0, *lead, slice(0, HALF))].astype(F32)).astype(stage.dtype)
        stage[1] = (get(d, 1) + came[(1, *lead, slice(HALF, OWN))].astype(F32)).astype(stage.dtype)

    def tree_last(came, second, get, own):
        lead = (slice(None),) * (len(came.shape) - 3)
        low = get(own, 0) + came[(1, *lead, slice(0, HALF))].astype(F32) + second[0].astype(F32)
        high = get(own, 1) + came[(0, *lead, slice(HALF, OWN))].astype(F32) + second[1].astype(F32)
        return low, high

    def halves(h):
        return slice(h * HALF, (h + 1) * HALF)

    def get_x(r):
        return lambda y_, h: px[r, a * 4 + y_, halves(h)]

    def get_y(r):
        return lambda y_, h: py[r, :, y_, halves(h)]

    def get_z(r):
        return lambda z_, h: acc[r, :, z_, halves(h)]

    def constant_terms(r, h, value, first):
        blocks = value.shape[-1] // 128
        total = jnp.zeros((HALF, 128), F32)
        for j in range(blocks):
            row = c * (half // 128) + first + j
            part = value[:, j * 128 : (j + 1) * 128]
            total = total + jnp.maximum(part, 0.0) * tab[3, pl.ds(row, 1), :]
            total = total + jnp.minimum(part, 0.0) * tab[4, pl.ds(row, 1), :]
        oacc[h, r] += total

    def step_lam(r):
        pick_rows(r)
        if r == 0:
            pl.semaphore_wait(barrier, 5 + len(by_z))
            load_tx.wait()
            send("dx", 0, dt.at[pl.ds(0, cx)], dn.at[pl.ds(0, cx), its], twin)
            load_ro.wait()
        lam_rows(r)
        send("lam", r, lam.at[r, :, mine], lam.at[r, :, its], twin)
        if r == 0:
            load_ty.wait()
            send("dy", 0, dt.at[pl.ds(cx, cy)], dn.at[pl.ds(cx, cy), its], twin)

    def times_down(r, units):
        return lax.dot_general(lam[r], dn[units, :], NT, preferred_element_type=F32)

    def step_downx(r):
        if r == 0:
            load_dx.wait()
            arrive("dx", 0)
        arrive("lam", r)
        for n in range(cx // 256):
            columns = slice(n * 256, (n + 1) * 256)
            px[r, :, :, columns] = times_down(r, columns).reshape(8, OWN, 256)
        x1s[r] = px[r, pl.ds((1 - a) * 4, 4)].astype(BF16)
        send("x1", r, x1s.at[r], x1r.at[r], other_x)

    def step_downy(r):
        if r == 0:
            load_up.start()
            load_gate.start()
            load_dy.wait()
            arrive("dy", 0)
        for n in range(cy // 256):
            columns = slice(n * 256, (n + 1) * 256)
            units = slice(cx + n * 256, cx + (n + 1) * 256)
            py[r, :, :, :, columns] = times_down(r, units).reshape(2, 4, OWN, 256)
        tree_first(yps.at[r], get_y(r), yu, yd, yo)
        send("yu1", r, yps.at[r, 0], ypr.at[r, 0], up_y)
        send("yd1", r, yps.at[r, 1], ypr.at[r, 1], down_y)

    def step_x1(r):
        arrive("x1", r)
        own = pl.ds(a * 4, 4)
        px[r, own] += x1r[r].astype(F32)
        tree_first(xps.at[r], get_x(r), yu, yd, yo)
        send("xu1", r, xps.at[r, 0], xpr.at[r, 0], up_y)
        send("xd1", r, xps.at[r, 1], xpr.at[r, 1], down_y)

    def step_y1(r):
        arrive("yu1", r)
        arrive("yd1", r)
        tree_second(yqs.at[r], ypr.at[r], get_y(r), yu, yd)
        send("yu2", r, yqs.at[r, 0], yqr.at[r, 0], up_y)
        send("yd2", r, yqs.at[r, 1], yqr.at[r, 1], down_y)

    def step_x2(r):
        arrive("xu1", r)
        arrive("xd1", r)
        tree_second(xqs.at[r], xpr.at[r], get_x(r), yu, yd)
        send("xu2", r, xqs.at[r, 0], xqr.at[r, 0], up_y)
        send("xd2", r, xqs.at[r, 1], xqr.at[r, 1], down_y)

    def step_y2(r):
        arrive("yu2", r)
        arrive("yd2", r)
        low, high = tree_last(ypr.at[r], yqr.at[r], get_y(r), y)
        py[r, :, y, halves(0)] = low
        py[r, :, y, halves(1)] = high
        yxs[r] = py[r, 1 - a, y].astype(BF16)
        send("yx", r, yxs.at[r], yxr.at[r], other_x)

    def step_x3(r):
        arrive("xu2", r)
        arrive("xd2", r)
        for h, value in enumerate(tree_last(xpr.at[r], xqr.at[r], get_x(r), y)):
            lx[r, c, a, y, halves(h)] = value.astype(BF16)
            constant_terms(r, h, value, 0)
        block = lx.at[r, c, a, y]
        send("gxu1", r, block, block, up_y)
        send("gxd1", r, block, block, down_y)
        send("gxx0", r, block, block, other_x)
        if r in SPREAD:
            send("gxo", r, block, block, over_y)

    def step_y3(r):
        arrive("yx", r)
        for h in range(2):
            value = py[r, a, y, halves(h)] + yxr[r, halves(h)].astype(F32)
            ly[r, c, a, y, halves(h)] = value.astype(BF16)
            constant_terms(r, h, value, cx // 128)
        block = ly.at[r, c, a, y]
        send("gyx", r, block, block, other_x)
        send("gyu1", r, block, block, up_y)
        send("gyd1", r, block, block, down_y)
        if r in SPREAD:
            send("gyo", r, block, block, over_y)

    def step_gx1(r):
        arrive("gxu1", r)
        arrive("gxd1", r)
        if r in SPREAD:
            arrive("gxo", r)
            for name, y_ in (("gxx1", yu), ("gxx2", yd), ("gxx3", yo)):
                block = lx.at[r, c, a, y_]
                send(name, r, block, block, other_x)
            block = lx.at[r, c, a]
            send("tx0", r, block, block, twin)
            return
        below = lx.at[r, c, a, yd, halves(0)]
        above = lx.at[r, c, a, yu, halves(1)]
        send("gxu2", r, below, below, up_y)
        send("gxd2", r, above, above, down_y)
        for name, y_ in (("gxx1", yu), ("gxx2", yd)):
            block = lx.at[r, c, a, y_]
            send(name, r, block, block, other_x)

    def step_gy1(r):
        arrive("gyx", r)
        block = ly.at[r, c, :, y]
        send("ty0", r, block, block, twin)
        block = ly.at[r, c, 1 - a, y]
        send("gyu1b", r, block, block, up_y)
        send("gyd1b", r, block, block, down_y)
        if r in SPREAD:
            send("gyob", r, block, block, over_y)

    def step_gx2(r):
        arrive("gxu2", r)
        arrive("gxd2", r)
        block = lx.at[r, c, a, yo]
        send("gxx3", r, block, block, other_x)
        block = lx.at[r, c, a]
        send("tx0", r, block, block, twin)

    def step_gy2(r):
        for name in ("gyu1", "gyd1", "gyu1b", "gyd1b"):
            arrive(name, r)
        below = ly.at[r, c, :, yd, halves(0)]
        above = ly.at[r, c, :, yu, halves(1)]
        send("gyu2", r, below, below, up_y)
        send("gyd2", r, above, above, down_y)
        for name, y_ in (("ty1", yu), ("ty2", yd)):
            block = ly.at[r, c, :, y_]
            send(name, r, block, block, twin)

    def step_gx3(r):
        for k in range(4):
            arrive("gxx%d" % k, r)
        block = lx.at[r, c, 1 - a]
        send("tx1", r, block, block, twin)

    def step_gy3(r):
        if r in SPREAD:
            for name in ("gyu1", "gyd1", "gyu1b", "gyd1b", "gyo", "gyob"):
                arrive(name, r)
        else:
            arrive("gyu2", r)
            arrive("gyd2", r)
        for name, y_ in (("ty1", yu), ("ty2", yd), ("ty3", yo)) if r in SPREAD else (("ty3", yo),):
            block = ly.at[r, c, :, y_]
            send(name, r, block, block, twin)

    def times_weights(r, cc, kinds, add):
        base = cc * half
        columns_x = pl.ds(pl.multiple_of(base, 256), cx)
        columns_y = pl.ds(pl.multiple_of(base + cx, 256), cy)

        def block(n, carry):
            units = pl.ds(pl.multiple_of(n * 256, 256), 256)
            total = None
            for ref, columns in ((lx, columns_x), (ly, columns_y))[kinds]:
                value = ref[r, cc].reshape(rows, columns.size)
                for part, weight in ((jnp.maximum(value, 0), wp), (jnp.minimum(value, 0), wn)):
                    term = lax.dot_general(part, weight[units, columns], NT, preferred_element_type=F32)
                    total = term if total is None else total + term
            total = total.reshape(2, 4, OWN, 256)
            if add:
                acc[r, :, :, :, units] += total
            else:
                acc[r, :, :, :, units] = total
            return carry

        lax.fori_loop(0, d_own // 256, block, 0, unroll=True)

    def step_mma(r):
        times_weights(r, c, slice(0, 2), False)

    def step_mm(r):
        arrive("tx0", r)
        arrive("tx1", r)
        times_weights(r, 1 - c, slice(0, 1), True)
        for k in range(4):
            arrive("ty%d" % k, r)
        times_weights(r, 1 - c, slice(1, 2), True)
        if r in STRAIGHT:
            k = STRAIGHT.index(r)
            ends[k] = acc[r].astype(BF16)
            for (s, f), device in by_z.items():
                send("e%d%d" % (s, f), r, ends.at[k, (xh + f) % 2, (z + s) % 4], endr.at[k, s * 2 + f], device)
        else:
            for s, z_ in ((1, zu), (3, zd), (2, zo)):
                send("z%d" % s, r, acc.at[r, :, z_], zr.at[r, s - 1], by_z[s, 0])

    def step_z1(r):
        for s in (1, 3, 2):
            arrive("z%d" % s, r)
        hs[r] = (acc[r, 1 - xh, z] + zr[r, 0, 1 - xh]) + (zr[r, 1, 1 - xh] + zr[r, 2, 1 - xh])
        send("h", r, hs.at[r], hr.at[r], other_h)

    def drain(keys):
        for key in keys:
            unsent.pop(key).wait_send()

    def step_out(r):
        if r == CHUNKS - 1:
            drain(tuple(key for key in unsent if key[0][0] not in "hez"))
        first = pl.multiple_of((xh * 4 + z) * OWN, OWN)
        total = lam[r, pl.ds(first, OWN), 0:d_own].astype(F32) + acc[r, xh, z]
        if r in STRAIGHT:
            for s, f in by_z:
                arrive("e%d%d" % (s, f), r)
                total = total + endr[STRAIGHT.index(r), s * 2 + f].astype(F32)
        else:
            total = total + (zr[r, 0, xh] + zr[r, 1, xh] + zr[r, 2, xh])
            arrive("h", r)
            total = total + hr[r]
        for h in range(2):
            out[h * 64 + r * HALF : h * 64 + (r + 1) * HALF, :] = total[halves(h)]

    def weights(k):
        if k == 0:
            load_up.wait()
            load_gate.wait()

        def block(j, carry):
            columns = pl.ds(pl.multiple_of(j * 128, 128), 128)
            scaled = wp[:, columns].astype(F32) * tab[0, pl.ds(j, 1), :]
            gates = wn[:, columns].astype(F32)
            wp[:, columns] = (scaled + gates * tab[1, pl.ds(j, 1), :]).astype(BF16)
            wn[:, columns] = (scaled + gates * tab[2, pl.ds(j, 1), :]).astype(BF16)
            return carry

        count = wp.shape[1] // 128 // 2
        lax.fori_loop(k * count, (k + 1) * count, block, 0)

    partners = (
        twin,
        at(z + 1 - 2 * (z % 2), xh, y, a, c),
        at(3 - z, xh, y, a, c),
        other_h,
    )

    def offset_start():
        obs[0] = jnp.broadcast_to(jnp.sum(oacc[...].reshape(128, 128).T, axis=0, keepdims=True), (8, 128))
        send("o", 0, obs.at[0], obr.at[0], partners[0])

    def offset_step(k):
        if k == 0:
            offset_start()
            return
        arrive("o", k - 1)
        if k < 4:
            obs[k] = obs[k - 1] + obr[k - 1]
            send("o", k, obs.at[k], obr.at[k], partners[k])
        else:
            total = obs[k - 1] + obr[k - 1]
            off[...] = jnp.where(c == 0, total[0:1, 0:64], total[0:1, 64:128])

    table = dict(
        lam=step_lam, downx=step_downx, downy=step_downy, x1=step_x1, y1=step_y1, x2=step_x2, y2=step_y2,
        x3=step_x3, y3=step_y3, gx1=step_gx1, gy1=step_gy1, gx2=step_gx2, gy2=step_gy2, gx3=step_gx3, gy3=step_gy3,
        mma=step_mma, mm=step_mm, z1=step_z1, out=step_out, w=weights, o=offset_step,
    )
    for name, r in PLAN:
        table[name](r)
    drain(tuple(unsent))


def hand_over(coeffs, offsets, out, off):
    out[...] = coeffs[...]
    off[...] = offsets[...]


def per_device(
    spec_rows, readout, gate_weight, up_weight, down_weight, gate_lo, gate_width, up_lo, up_width, flags
):
    d_own = readout.shape[1]
    units = down_weight.shape[0]
    half = units // 2
    cx = 768
    cy = half - cx
    rows = 8 * OWN
    r = CHUNKS
    lanes = [value.reshape(units // 128, 128) for value in (gate_lo, gate_width, up_lo, up_width, flags)]
    vm = pltpu.VMEM
    scratch = [
        vm((readout.shape[0], d_own), BF16),
        vm((d_own, units), BF16),
        vm((d_own, units), BF16),
        vm((half, 2 * d_own), BF16),
        vm((half, d_own), BF16),
        vm((spec_rows.shape[0], 8), F32),
        vm((rows, readout.shape[0]), BF16),
        vm((r, rows, 2 * d_own), BF16),
        vm((5, 32, 128), F32),
        vm((r, 8, OWN, cx), F32),
        vm((r, 2, 4, OWN, cy), F32),
        vm((r, 4, OWN, cx), BF16),
        vm((r, 4, OWN, cx), BF16),
        vm((r, 2, OWN, cx), BF16),
        vm((r, 2, OWN, cx), BF16),
        vm((r, 2, HALF, cx), BF16),
        vm((r, 2, HALF, cx), BF16),
        vm((r, 2, 2, OWN, cy), BF16),
        vm((r, 2, 2, OWN, cy), BF16),
        vm((r, 2, 2, HALF, cy), BF16),
        vm((r, 2, 2, HALF, cy), BF16),
        vm((r, OWN, cy), BF16),
        vm((r, OWN, cy), BF16),
        vm((r, 2, 2, 4, OWN, cx), BF16),
        vm((r, 2, 2, 4, OWN, cy), BF16),
        vm((r, 2, 4, OWN, d_own), F32),
        vm((r, 3, 2, OWN, d_own), F32),
        vm((r, OWN, d_own), F32),
        vm((r, OWN, d_own), F32),
        vm((len(STRAIGHT), 2, 4, OWN, d_own), BF16),
        vm((len(STRAIGHT), 8, OWN, d_own), BF16),
        vm((2, r, HALF, 128), F32),
        vm((4, 8, 128), F32),
        vm((4, 8, 128), F32),
        pltpu.SemaphoreType.DMA((7,)),
        pltpu.SemaphoreType.DMA((104,)),
        pltpu.SemaphoreType.DMA((172,)),
    ]
    held = pl.BlockSpec(memory_space=pltpu.VMEM)
    far = pl.BlockSpec(memory_space=pl.ANY)
    coeffs, offsets = pl.pallas_call(
        kernel,
        name="bound_pass",
        out_shape=(
            jax.ShapeDtypeStruct((spec_rows.shape[0] // 8, d_own), F32),
            jax.ShapeDtypeStruct((1, 64), F32),
        ),
        in_specs=[held, far, far, far, far, held, held, held, held, held],
        out_specs=(held, held),
        scratch_shapes=scratch,
        compiler_params=pltpu.CompilerParams(
            collective_id=0, has_side_effects=True, vmem_limit_bytes=60 * 1024 * 1024
        ),
    )(spec_rows.T, readout, gate_weight, up_weight, down_weight, *lanes)
    coeffs, offsets = pl.pallas_call(
        hand_over,
        name="hand_over",
        out_shape=(jax.ShapeDtypeStruct(coeffs.shape, F32), jax.ShapeDtypeStruct(offsets.shape, F32)),
        in_specs=[held, held],
        out_specs=(held, held),
    )(coeffs, offsets)
    return coeffs, offsets.reshape(64)


def solution(mesh):
    placed = (
        P(),
        P(None, "wid"),
        P("wid", "hid"),
        P("wid", "hid"),
        P("hid", "wid"),
        P("hid"),
        P("hid"),
        P("hid"),
        P("hid"),
        P("hid"),
    )
    return jax.shard_map(
        per_device,
        mesh=mesh,
        in_specs=placed,
        out_specs=(P("hid", "wid"), P("wid")),
        check_vma=False,
    )
```

```python
import jax
import jax.numpy as jnp
from jax import lax
from jax.experimental import pallas as pl
from jax.experimental.pallas import tpu as pltpu
from jax.sharding import PartitionSpec as P

MESH = pl.DeviceIdType.MESH
F32 = jnp.float32
BF16 = jnp.bfloat16
NT = (((1,), (1,)), ((), ()))

CHUNKS = 4
OWN = 32
HALF = OWN // 2


def silu(value):
    return value / (1.0 + jnp.exp(-value))


def unit_tables(gate_lo, gate_width, up_lo, up_width, flags):
    gate_hi = gate_lo + gate_width
    up_hi = up_lo + up_width
    middle = 0.5 * (gate_lo + gate_hi)
    valley = jnp.clip(-1.2784645, gate_lo, gate_hi)
    silu_lo = silu(gate_lo)
    silu_hi = silu(gate_hi)
    silu_valley = silu(valley)
    s_low = jnp.minimum(jnp.minimum(silu_lo, silu_hi), silu_valley)
    s_high = jnp.maximum(silu_lo, silu_hi)
    slope = (silu_hi - silu_lo) / gate_width
    rest_a = silu_lo - slope * gate_lo
    rest_b = silu(middle) - slope * middle
    rest_c = silu_valley - slope * valley
    b_low = jnp.minimum(jnp.minimum(rest_a, rest_b), rest_c)
    b_high = jnp.maximum(jnp.maximum(rest_a, rest_b), rest_c)
    second = flags == 1
    as_lower = jnp.where(second, up_hi, up_lo)
    as_upper = jnp.where(second, up_lo, up_hi)
    au = jnp.where(second, s_high, s_low)
    kp = jnp.maximum(as_lower, 0.0) * b_low + jnp.minimum(as_lower, 0.0) * b_high - au * as_lower
    kn = jnp.minimum(as_upper, 0.0) * b_low + jnp.maximum(as_upper, 0.0) * b_high - au * as_upper
    return au, as_lower * slope, as_upper * slope, kp, kn


PLAN = (
    ("lam", 0), ("lam", 1), ("downx", 0), ("downy", 0), ("lam", 2), ("downx", 1), ("downy", 1), ("y1", 0),
    ("downx", 2), ("downy", 2), ("lam", 3), ("x1", 0), ("y2", 0), ("y1", 1), ("x1", 1), ("downx", 3), ("x2", 0),
    ("y1", 2), ("x1", 2), ("downy", 3), ("x3", 0), ("x2", 1), ("y2", 2), ("y2", 1), ("x2", 2), ("x1", 3),
    ("x3", 1), ("x3", 2), ("y3", 2), ("w", 0), ("gx1", 0), ("y3", 0), ("y1", 3), ("x2", 3), ("gx1", 2), ("gy1", 2),
    ("y3", 1), ("x3", 3), ("gy1", 0), ("y2", 3), ("gx1", 1), ("w", 1), ("gy1", 1), ("gx2", 2), ("gx2", 1),
    ("gy2", 2), ("gy2", 0), ("gx2", 0), ("y3", 3), ("o", 0), ("gx3", 2), ("gy3", 2), ("gy2", 1), ("gx1", 3),
    ("o", 1), ("mma", 2), ("gx3", 0), ("gy1", 3), ("gy3", 0), ("mm", 2), ("mma", 0), ("gy3", 1), ("mm", 0),
    ("gx3", 1), ("mma", 1), ("gy3", 3), ("mm", 1), ("gx3", 3), ("o", 2), ("mma", 3), ("mm", 3), ("o", 3),
    ("out", 2), ("out", 0), ("out", 1), ("o", 4), ("out", 3),
)
STRAIGHT = (0, 1, 2, 3)
SPREAD = (3,)


def kernel(
    spec, readout, gate, up, down, gate_lo, gate_width, up_lo, up_width, flags,
    out, off,
    ro, wp, wn, dn, dt, pairs, oh, lam, tab,
    px, py, x1s, x1r, xps, xpr, xqs, xqr, yps, ypr, yqs, yqr, yxs, yxr,
    lx, ly, acc, zr, hs, hr, ends, endr, oacc, obs, obr,
    lsem, ssem, rsem,
):
    hid, wid = lax.axis_index("hid"), lax.axis_index("wid")
    z, xh = hid // 2, hid % 2
    y, a, c = wid // 4, (wid // 2) % 2, wid % 2
    half = dn.shape[0]
    cx, cy = px.shape[-1], py.shape[-1]
    d_own = ro.shape[1]
    rows = 8 * OWN
    mine, its = pl.ds(0, d_own), pl.ds(d_own, d_own)
    yu, yd, yo = (y + 1) % 4, (y + 3) % 4, (y + 2) % 4
    zu, zd, zo = (z + 1) % 4, (z + 3) % 4, (z + 2) % 4

    def at(z_, xh_, y_, a_, c_):
        return (z_ * 2 + xh_, (y_ * 2 + a_) * 2 + c_)

    up_y, down_y = at(z, xh, yu, a, c), at(z, xh, yd, a, c)
    other_x = at(z, xh, y, 1 - a, c)
    twin = at(z, xh, y, a, 1 - c)
    over_y = at(z, xh, yo, a, c)
    by_z = {(s, f): at((z + s) % 4, (xh + f) % 2, y, a, c) for s in range(4) for f in range(2) if s or f}
    other_h = by_z[0, 1]

    barrier = pltpu.get_barrier_semaphore()
    for device in (up_y, down_y, over_y, other_x, twin, *by_z.values()):
        pl.semaphore_signal(barrier, inc=1, device_id=device, device_id_type=MESH)

    load_ro = pltpu.make_async_copy(readout, ro, lsem.at[0])
    load_ro.start()
    my_half = pl.multiple_of(c * half, half)
    its_half = pl.multiple_of((1 - c) * half, half)
    load_dx = pltpu.make_async_copy(down.at[pl.ds(my_half, cx)], dn.at[pl.ds(0, cx), mine], lsem.at[1])
    load_dy = pltpu.make_async_copy(
        down.at[pl.ds(pl.multiple_of(my_half + cx, 256), cy)], dn.at[pl.ds(cx, cy), mine], lsem.at[2]
    )
    load_tx = pltpu.make_async_copy(down.at[pl.ds(its_half, cx)], dt.at[pl.ds(0, cx)], lsem.at[5])
    load_ty = pltpu.make_async_copy(
        down.at[pl.ds(pl.multiple_of(its_half + cx, 256), cy)], dt.at[pl.ds(cx, cy)], lsem.at[6]
    )
    load_tx.start()
    load_dx.start()
    load_ty.start()
    load_dy.start()
    load_up = pltpu.make_async_copy(up, wp, lsem.at[3])
    load_gate = pltpu.make_async_copy(gate, wn, lsem.at[4])

    copies = {}
    unsent = {}
    index = {}

    def send(name, r, src, dst, device):
        if (name, r - 2) in unsent:
            unsent.pop((name, r - 2)).wait_send()
        k = index.setdefault((name, r % 2), len(index))
        copy = pltpu.make_async_remote_copy(
            src_ref=src, dst_ref=dst, send_sem=ssem.at[k], recv_sem=rsem.at[len(copies)],
            device_id=device, device_id_type=MESH,
        )
        copy.start()
        copies[name, r] = unsent[name, r] = copy

    def arrive(name, r):
        copies[name, r].wait_recv()

    for k, table in enumerate(
        unit_tables(gate_lo[...], gate_width[...], up_lo[...], up_width[...], flags[...])
    ):
        tab[k, 0 : table.shape[0], :] = table

    tall = jnp.concatenate([spec[...].astype(F32), jnp.zeros((6, spec.shape[1]), F32)], axis=0)
    pairs[...] = tall.T
    oacc[...] = jnp.zeros_like(oacc)

    def pick_rows(r):
        def group(g, carry):
            a_, y_, co = g // 8, (g // 2) % 4, g % 2
            start = pl.multiple_of((y_ * 2 + a_) * 128 + co * 64 + r * 16, 16)
            pair = pairs[pl.ds(start, 16), :].astype(jnp.int32)
            classes = lax.broadcasted_iota(jnp.int32, (16, ro.shape[0]), 1)
            picked = jnp.where(classes == pair[:, 0:1], 1.0, 0.0) - jnp.where(classes == pair[:, 1:2], 1.0, 0.0)
            oh[pl.ds(pl.multiple_of(g * 16, 16), 16), :] = picked.astype(BF16)
            return carry

        lax.fori_loop(0, 16, group, 0)

    def lam_rows(r):
        lam[r, :, 0:d_own] = jnp.dot(oh[...], ro[...], preferred_element_type=F32).astype(BF16)

    def tree_first(stage, get, u, d, o):
        lead = (slice(None),) * (len(stage.shape) - 3)
        stage[(0, *lead, slice(0, HALF))] = get(o, 0).astype(stage.dtype)
        stage[(0, *lead, slice(HALF, OWN))] = get(u, 1).astype(stage.dtype)
        stage[(1, *lead, slice(0, HALF))] = get(d, 0).astype(stage.dtype)
        stage[(1, *lead, slice(HALF, OWN))] = get(o, 1).astype(stage.dtype)

    def tree_second(stage, came, get, u, d):
        lead = (slice(None),) * (len(came.shape) - 3)
        stage[0] = (get(u, 0) + came[(0, *lead, slice(0, HALF))].astype(F32)).astype(stage.dtype)
        stage[1] = (get(d, 1) + came[(1, *lead, slice(HALF, OWN))].astype(F32)).astype(stage.dtype)

    def tree_last(came, second, get, own):
        lead = (slice(None),) * (len(came.shape) - 3)
        low = get(own, 0) + came[(1, *lead, slice(0, HALF))].astype(F32) + second[0].astype(F32)
        high = get(own, 1) + came[(0, *lead, slice(HALF, OWN))].astype(F32) + second[1].astype(F32)
        return low, high

    def halves(h):
        return slice(h * HALF, (h + 1) * HALF)

    def get_x(r):
        return lambda y_, h: px[r, a * 4 + y_, halves(h)]

    def get_y(r):
        return lambda y_, h: py[r, :, y_, halves(h)]

    def get_z(r):
        return lambda z_, h: acc[r, :, z_, halves(h)]

    def constant_terms(r, h, value, first):
        blocks = value.shape[-1] // 128
        total = jnp.zeros((HALF, 128), F32)
        for j in range(blocks):
            row = c * (half // 128) + first + j
            part = value[:, j * 128 : (j + 1) * 128]
            total = total + jnp.maximum(part, 0.0) * tab[3, pl.ds(row, 1), :]
            total = total + jnp.minimum(part, 0.0) * tab[4, pl.ds(row, 1), :]
        oacc[h, r] += total

    def step_lam(r):
        pick_rows(r)
        if r == 0:
            pl.semaphore_wait(barrier, 5 + len(by_z))
            load_tx.wait()
            send("dx", 0, dt.at[pl.ds(0, cx)], dn.at[pl.ds(0, cx), its], twin)
            load_ro.wait()
        lam_rows(r)
        send("lam", r, lam.at[r, :, mine], lam.at[r, :, its], twin)
        if r == 0:
            load_ty.wait()
            send("dy", 0, dt.at[pl.ds(cx, cy)], dn.at[pl.ds(cx, cy), its], twin)

    def times_down(r, units):
        return lax.dot_general(lam[r], dn[units, :], NT, preferred_element_type=F32)

    def step_downx(r):
        if r == 0:
            load_dx.wait()
            arrive("dx", 0)
        arrive("lam", r)
        for n in range(cx // 256):
            columns = slice(n * 256, (n + 1) * 256)
            px[r, :, :, columns] = times_down(r, columns).reshape(8, OWN, 256)
        x1s[r] = px[r, pl.ds((1 - a) * 4, 4)].astype(BF16)
        send("x1", r, x1s.at[r], x1r.at[r], other_x)

    def step_downy(r):
        if r == 0:
            load_up.start()
            load_gate.start()
            load_dy.wait()
            arrive("dy", 0)
        for n in range(cy // 256):
            columns = slice(n * 256, (n + 1) * 256)
            units = slice(cx + n * 256, cx + (n + 1) * 256)
            py[r, :, :, :, columns] = times_down(r, units).reshape(2, 4, OWN, 256)
        tree_first(yps.at[r], get_y(r), yu, yd, yo)
        send("yu1", r, yps.at[r, 0], ypr.at[r, 0], up_y)
        send("yd1", r, yps.at[r, 1], ypr.at[r, 1], down_y)

    def step_x1(r):
        arrive("x1", r)
        own = pl.ds(a * 4, 4)
        px[r, own] += x1r[r].astype(F32)
        tree_first(xps.at[r], get_x(r), yu, yd, yo)
        send("xu1", r, xps.at[r, 0], xpr.at[r, 0], up_y)
        send("xd1", r, xps.at[r, 1], xpr.at[r, 1], down_y)

    def step_y1(r):
        arrive("yu1", r)
        arrive("yd1", r)
        tree_second(yqs.at[r], ypr.at[r], get_y(r), yu, yd)
        send("yu2", r, yqs.at[r, 0], yqr.at[r, 0], up_y)
        send("yd2", r, yqs.at[r, 1], yqr.at[r, 1], down_y)

    def step_x2(r):
        arrive("xu1", r)
        arrive("xd1", r)
        tree_second(xqs.at[r], xpr.at[r], get_x(r), yu, yd)
        send("xu2", r, xqs.at[r, 0], xqr.at[r, 0], up_y)
        send("xd2", r, xqs.at[r, 1], xqr.at[r, 1], down_y)

    def step_y2(r):
        arrive("yu2", r)
        arrive("yd2", r)
        low, high = tree_last(ypr.at[r], yqr.at[r], get_y(r), y)
        py[r, :, y, halves(0)] = low
        py[r, :, y, halves(1)] = high
        yxs[r] = py[r, 1 - a, y].astype(BF16)
        send("yx", r, yxs.at[r], yxr.at[r], other_x)

    def step_x3(r):
        arrive("xu2", r)
        arrive("xd2", r)
        for h, value in enumerate(tree_last(xpr.at[r], xqr.at[r], get_x(r), y)):
            lx[r, c, a, y, halves(h)] = value.astype(BF16)
            constant_terms(r, h, value, 0)
        block = lx.at[r, c, a, y]
        send("gxu1", r, block, block, up_y)
        send("gxd1", r, block, block, down_y)
        send("gxx0", r, block, block, other_x)
        if r in SPREAD:
            send("gxo", r, block, block, over_y)

    def step_y3(r):
        arrive("yx", r)
        for h in range(2):
            value = py[r, a, y, halves(h)] + yxr[r, halves(h)].astype(F32)
            ly[r, c, a, y, halves(h)] = value.astype(BF16)
            constant_terms(r, h, value, cx // 128)
        block = ly.at[r, c, a, y]
        send("gyx", r, block, block, other_x)
        send("gyu1", r, block, block, up_y)
        send("gyd1", r, block, block, down_y)
        if r in SPREAD:
            send("gyo", r, block, block, over_y)

    def step_gx1(r):
        arrive("gxu1", r)
        arrive("gxd1", r)
        if r in SPREAD:
            arrive("gxo", r)
            for name, y_ in (("gxx1", yu), ("gxx2", yd), ("gxx3", yo)):
                block = lx.at[r, c, a, y_]
                send(name, r, block, block, other_x)
            block = lx.at[r, c, a]
            send("tx0", r, block, block, twin)
            return
        below = lx.at[r, c, a, yd, halves(0)]
        above = lx.at[r, c, a, yu, halves(1)]
        send("gxu2", r, below, below, up_y)
        send("gxd2", r, above, above, down_y)
        for name, y_ in (("gxx1", yu), ("gxx2", yd)):
            block = lx.at[r, c, a, y_]
            send(name, r, block, block, other_x)

    def step_gy1(r):
        arrive("gyx", r)
        block = ly.at[r, c, :, y]
        send("ty0", r, block, block, twin)
        block = ly.at[r, c, 1 - a, y]
        send("gyu1b", r, block, block, up_y)
        send("gyd1b", r, block, block, down_y)
        if r in SPREAD:
            send("gyob", r, block, block, over_y)

    def step_gx2(r):
        arrive("gxu2", r)
        arrive("gxd2", r)
        block = lx.at[r, c, a, yo]
        send("gxx3", r, block, block, other_x)
        block = lx.at[r, c, a]
        send("tx0", r, block, block, twin)

    def step_gy2(r):
        for name in ("gyu1", "gyd1", "gyu1b", "gyd1b"):
            arrive(name, r)
        below = ly.at[r, c, :, yd, halves(0)]
        above = ly.at[r, c, :, yu, halves(1)]
        send("gyu2", r, below, below, up_y)
        send("gyd2", r, above, above, down_y)
        for name, y_ in (("ty1", yu), ("ty2", yd)):
            block = ly.at[r, c, :, y_]
            send(name, r, block, block, twin)

    def step_gx3(r):
        for k in range(4):
            arrive("gxx%d" % k, r)
        block = lx.at[r, c, 1 - a]
        send("tx1", r, block, block, twin)

    def step_gy3(r):
        if r in SPREAD:
            for name in ("gyu1", "gyd1", "gyu1b", "gyd1b", "gyo", "gyob"):
                arrive(name, r)
        else:
            arrive("gyu2", r)
            arrive("gyd2", r)
        for name, y_ in (("ty1", yu), ("ty2", yd), ("ty3", yo)) if r in SPREAD else (("ty3", yo),):
            block = ly.at[r, c, :, y_]
            send(name, r, block, block, twin)

    def times_weights(r, cc, kinds, add):
        base = cc * half
        columns_x = pl.ds(pl.multiple_of(base, 256), cx)
        columns_y = pl.ds(pl.multiple_of(base + cx, 256), cy)

        def block(n, carry):
            units = pl.ds(pl.multiple_of(n * 256, 256), 256)
            total = None
            for ref, columns in ((lx, columns_x), (ly, columns_y))[kinds]:
                value = ref[r, cc].reshape(rows, columns.size)
                for part, weight in ((jnp.maximum(value, 0), wp), (jnp.minimum(value, 0), wn)):
                    term = lax.dot_general(part, weight[units, columns], NT, preferred_element_type=F32)
                    total = term if total is None else total + term
            total = total.reshape(2, 4, OWN, 256)
            if add:
                acc[r, :, :, :, units] += total
            else:
                acc[r, :, :, :, units] = total
            return carry

        lax.fori_loop(0, d_own // 256, block, 0, unroll=True)

    def step_mma(r):
        times_weights(r, c, slice(0, 2), False)

    def step_mm(r):
        arrive("tx0", r)
        arrive("tx1", r)
        times_weights(r, 1 - c, slice(0, 1), True)
        for k in range(4):
            arrive("ty%d" % k, r)
        times_weights(r, 1 - c, slice(1, 2), True)
        if r in STRAIGHT:
            k = STRAIGHT.index(r)
            ends[k] = acc[r].astype(BF16)
            for (s, f), device in by_z.items():
                send("e%d%d" % (s, f), r, ends.at[k, (xh + f) % 2, (z + s) % 4], endr.at[k, s * 2 + f], device)
        else:
            for s, z_ in ((1, zu), (3, zd), (2, zo)):
                send("z%d" % s, r, acc.at[r, :, z_], zr.at[r, s - 1], by_z[s, 0])

    def step_z1(r):
        for s in (1, 3, 2):
            arrive("z%d" % s, r)
        hs[r] = (acc[r, 1 - xh, z] + zr[r, 0, 1 - xh]) + (zr[r, 1, 1 - xh] + zr[r, 2, 1 - xh])
        send("h", r, hs.at[r], hr.at[r], other_h)

    def drain(keys):
        for key in keys:
            unsent.pop(key).wait_send()

    def step_out(r):
        if r == CHUNKS - 1:
            drain(tuple(key for key in unsent if key[0][0] not in "hez"))
        first = pl.multiple_of((xh * 4 + z) * OWN, OWN)
        total = lam[r, pl.ds(first, OWN), 0:d_own].astype(F32) + acc[r, xh, z]
        if r in STRAIGHT:
            for s, f in by_z:
                arrive("e%d%d" % (s, f), r)
                total = total + endr[STRAIGHT.index(r), s * 2 + f].astype(F32)
        else:
            total = total + (zr[r, 0, xh] + zr[r, 1, xh] + zr[r, 2, xh])
            arrive("h", r)
            total = total + hr[r]
        for h in range(2):
            out[h * 64 + r * HALF : h * 64 + (r + 1) * HALF, :] = total[halves(h)]

    def weights(k):
        if k == 0:
            load_up.wait()
            load_gate.wait()

        def block(j, carry):
            columns = pl.ds(pl.multiple_of(j * 128, 128), 128)
            scaled = wp[:, columns].astype(F32) * tab[0, pl.ds(j, 1), :]
            gates = wn[:, columns].astype(F32)
            wp[:, columns] = (scaled + gates * tab[1, pl.ds(j, 1), :]).astype(BF16)
            wn[:, columns] = (scaled + gates * tab[2, pl.ds(j, 1), :]).astype(BF16)
            return carry

        count = wp.shape[1] // 128 // 2
        lax.fori_loop(k * count, (k + 1) * count, block, 0)

    partners = (
        twin,
        at(z + 1 - 2 * (z % 2), xh, y, a, c),
        at(3 - z, xh, y, a, c),
        other_h,
    )

    def offset_start():
        obs[0] = jnp.broadcast_to(jnp.sum(oacc[...].reshape(128, 128).T, axis=0, keepdims=True), (8, 128))
        send("o", 0, obs.at[0], obr.at[0], partners[0])

    def offset_step(k):
        if k == 0:
            offset_start()
            return
        arrive("o", k - 1)
        if k < 4:
            obs[k] = obs[k - 1] + obr[k - 1]
            send("o", k, obs.at[k], obr.at[k], partners[k])
        else:
            total = obs[k - 1] + obr[k - 1]
            off[...] = jnp.where(c == 0, total[0:1, 0:64], total[0:1, 64:128])

    table = dict(
        lam=step_lam, downx=step_downx, downy=step_downy, x1=step_x1, y1=step_y1, x2=step_x2, y2=step_y2,
        x3=step_x3, y3=step_y3, gx1=step_gx1, gy1=step_gy1, gx2=step_gx2, gy2=step_gy2, gx3=step_gx3, gy3=step_gy3,
        mma=step_mma, mm=step_mm, z1=step_z1, out=step_out, w=weights, o=offset_step,
    )
    for name, r in PLAN:
        table[name](r)
    drain(tuple(unsent))


def hand_over(coeffs, offsets, out, off):
    out[...] = coeffs[...]
    off[...] = offsets[...]


def per_device(
    spec_rows, readout, gate_weight, up_weight, down_weight, gate_lo, gate_width, up_lo, up_width, flags
):
    d_own = readout.shape[1]
    units = down_weight.shape[0]
    half = units // 2
    cx = 768
    cy = half - cx
    rows = 8 * OWN
    r = CHUNKS
    lanes = [value.reshape(units // 128, 128) for value in (gate_lo, gate_width, up_lo, up_width, flags)]
    vm = pltpu.VMEM
    scratch = [
        vm((readout.shape[0], d_own), BF16),
        vm((d_own, units), BF16),
        vm((d_own, units), BF16),
        vm((half, 2 * d_own), BF16),
        vm((half, d_own), BF16),
        vm((spec_rows.shape[0], 8), F32),
        vm((rows, readout.shape[0]), BF16),
        vm((r, rows, 2 * d_own), BF16),
        vm((5, 32, 128), F32),
        vm((r, 8, OWN, cx), F32),
        vm((r, 2, 4, OWN, cy), F32),
        vm((r, 4, OWN, cx), BF16),
        vm((r, 4, OWN, cx), BF16),
        vm((r, 2, OWN, cx), BF16),
        vm((r, 2, OWN, cx), BF16),
        vm((r, 2, HALF, cx), BF16),
        vm((r, 2, HALF, cx), BF16),
        vm((r, 2, 2, OWN, cy), BF16),
        vm((r, 2, 2, OWN, cy), BF16),
        vm((r, 2, 2, HALF, cy), BF16),
        vm((r, 2, 2, HALF, cy), BF16),
        vm((r, OWN, cy), BF16),
        vm((r, OWN, cy), BF16),
        vm((r, 2, 2, 4, OWN, cx), BF16),
        vm((r, 2, 2, 4, OWN, cy), BF16),
        vm((r, 2, 4, OWN, d_own), F32),
        vm((r, 3, 2, OWN, d_own), F32),
        vm((r, OWN, d_own), F32),
        vm((r, OWN, d_own), F32),
        vm((len(STRAIGHT), 2, 4, OWN, d_own), BF16),
        vm((len(STRAIGHT), 8, OWN, d_own), BF16),
        vm((2, r, HALF, 128), F32),
        vm((4, 8, 128), F32),
        vm((4, 8, 128), F32),
        pltpu.SemaphoreType.DMA((7,)),
        pltpu.SemaphoreType.DMA((104,)),
        pltpu.SemaphoreType.DMA((172,)),
    ]
    held = pl.BlockSpec(memory_space=pltpu.VMEM)
    far = pl.BlockSpec(memory_space=pl.ANY)
    coeffs, offsets = pl.pallas_call(
        kernel,
        name="bound_pass",
        out_shape=(
            jax.ShapeDtypeStruct((spec_rows.shape[0] // 8, d_own), F32),
            jax.ShapeDtypeStruct((1, 64), F32),
        ),
        in_specs=[held, far, far, far, far, held, held, held, held, held],
        out_specs=(held, held),
        scratch_shapes=scratch,
        compiler_params=pltpu.CompilerParams(
            collective_id=0, has_side_effects=True, vmem_limit_bytes=60 * 1024 * 1024
        ),
    )(spec_rows.T, readout, gate_weight, up_weight, down_weight, *lanes)
    coeffs, offsets = pl.pallas_call(
        hand_over,
        name="hand_over",
        out_shape=(jax.ShapeDtypeStruct(coeffs.shape, F32), jax.ShapeDtypeStruct(offsets.shape, F32)),
        in_specs=[held, held],
        out_specs=(held, held),
    )(coeffs, offsets)
    return coeffs, offsets.reshape(64)


def solution(mesh):
    placed = (
        P(),
        P(None, "wid"),
        P("wid", "hid"),
        P("wid", "hid"),
        P("hid", "wid"),
        P("hid"),
        P("hid"),
        P("hid"),
        P("hid"),
        P("hid"),
    )
    return jax.shard_map(
        per_device,
        mesh=mesh,
        in_specs=placed,
        out_specs=(P("hid", "wid"), P("wid")),
        check_vma=False,
    )
```
